256 devices in a mesh: space: 32 (over y, z_hi, core), slab: 8 (over x, z_lo).
Axes of the slice: x: 4, y: 4, z: 8 (z_hi: 4, z_lo: 2; z = z_hi * 2 + z_lo), core: 2. Of those that a mesh axis runs over, the one named last changes fastest.
Arguments:
- latents: bfloat16 [131072, 512], P(('space', 'slab')), may hold values from -6 to 6
- upstream: bfloat16 [131072, 512], P(('space', 'slab')), may hold values from -6 to 6
- msg_weight: bfloat16 [2, 512, 512], replicated, may hold values from -0.25 to 0.25
- self_weight: bfloat16 [2, 512, 512], replicated, may hold values from -0.25 to 0.25
- agg_weight: bfloat16 [2, 512, 512], replicated, may hold values from -0.25 to 0.25
- out_weight: bfloat16 [2, 512, 512], replicated, may hold values from -0.25 to 0.25
- gains: float32 [2, 512], replicated, may hold values from 0.25 to 1.75
- edge_weight: bfloat16 [1024, 6, 128, 128], P(('space', 'slab')), as said below
- nbr_slot: int32 [1024, 6], P(('space', 'slab')), may hold values from 0 to 11, as said below
- send_list: int32 [32, 8, 4, 2], P('space', 'slab'), may hold values from 0 to 3, as said below
Outputs:
- latents_out: bfloat16 [131072, 512], P(('space', 'slab'))
- latent_grad: float32 [131072, 512], P(('space', 'slab'))
- grad_msg: float32 [2, 512, 512], P(None, 'space')
- grad_self: float32 [2, 512, 512], P(None, 'space')
- grad_agg: float32 [2, 512, 512], P(None, 'space')
- grad_out: float32 [2, 512, 512], P(None, 'space')
- grad_gain: float32 [2, 512], P(None, 'space')
The draws below stay inside these ranges and needn't reach their ends.
Inputs may be any that keep to these rules, and one draw needn't show every extreme that they name: `nbr_slot`: entry [b, k] indexes the extended list of block b's device: 0 to 3 its own blocks, then 2 entries each from the lower and upper space neighbour and the lower and upper slab neighbour, in that order; entries of a missing neighbour are never named. `send_list`: entry [s, l, d, t] is a local block index that device (s, l) sends: d = 0 to space index s + 1, d = 1 to s - 1, d = 2 to slab index l + 1, d = 3 to l - 1; the 2 entries of one row are distinct. `edge_weight`: tile [b, k] has the rows of block b as first index and the rows of the source block as second index.
All inputs are finite; a program needn't handle non-finite values.
Results may differ from the reference program's by a relative error of at most 0.039.
Values may be sent and summed in bfloat16 or wider, within the bound.
A program may use at most 128 MiB of HBM per device.

```python
import jax
import jax.numpy as jnp
from jax import lax

W = 512
BLOCK = 128
B_DEV = 4
K = 6
LAYERS = 2
HALO = 2
SLOTS = 12
BLOCKS = 1024
NODES = 131072
N_SPACE = 32
N_SLAB = 8


def draw_edge_weight(key, part):
    key = jax.random.fold_in(key, 13)
    keys = jax.random.split(key, 2)
    shape = (BLOCKS, K, BLOCK, BLOCK)
    keep = jax.random.bernoulli(keys[0], 0.25, shape)
    values = jax.random.normal(keys[1], shape, jnp.float32) * 0.09
    return jnp.where(keep, values, 0.0).astype(jnp.bfloat16)


def draw_nbr_slot(key, part):
    key = jax.random.fold_in(key, 12)
    keys = jax.random.split(key, 3)
    index = jnp.arange(BLOCKS, dtype=jnp.int32)
    device = index // B_DEV
    local = index % B_DEV
    space_pos = device // N_SLAB
    slab_pos = device % N_SLAB
    present = jnp.stack([space_pos > 0, space_pos < N_SPACE - 1, slab_pos > 0, slab_pos < N_SLAB - 1], axis=1)
    own_pick = jax.random.randint(keys[0], (BLOCKS, 5), 0, B_DEV)
    columns = [local]
    for direction in range(4):
        halo_slot = B_DEV + direction * HALO + local % HALO
        columns.append(jnp.where(present[:, direction], halo_slot, own_pick[:, direction]))
    direction_pick = jax.random.randint(keys[1], (BLOCKS,), 0, 5)
    offset = jax.random.randint(keys[2], (BLOCKS,), 0, HALO)
    usable = jnp.concatenate([jnp.ones((BLOCKS, 1), dtype=bool), present], axis=1)
    chosen_ok = jnp.take_along_axis(usable, direction_pick[:, None], axis=1)[:, 0]
    extra = jnp.where((direction_pick > 0) & chosen_ok, B_DEV + (direction_pick - 1) * HALO + offset, own_pick[:, 4])
    columns.append(extra)
    return jnp.stack(columns, axis=1).astype(jnp.int32)


def draw_send_list(key, part):
    key = jax.random.fold_in(key, 11)
    scores = jax.random.randint(key, (N_SPACE, N_SLAB, 4, B_DEV), 0, 1 << 20) * B_DEV + jnp.arange(B_DEV, dtype=jnp.int32)
    order = jnp.argsort(scores, axis=-1)
    return order[..., :HALO].astype(jnp.int32)


def shard_levels(own_key, dims, cuts, smallest, largest):
    def one(dim, blocks):
        steps = jax.random.uniform(jax.random.fold_in(jax.random.fold_in(own_key, 6), dim), (blocks,), jnp.float32, smallest / len(cuts), largest / len(cuts))
        return jnp.repeat(jnp.exp(steps), dims[dim] // blocks).reshape((-1,) + (1,) * (len(dims) - dim - 1))

    factor_of = one(*cuts[0])
    for cut in cuts[1:]:
        factor_of = factor_of * one(*cut)
    return factor_of


def normal_values(key, extent, spread, most, shards=(), kind=jnp.bfloat16):
    drawn = spread * jax.random.normal(key, extent, jnp.float32)
    if shards:
        drawn = drawn * shard_levels(key, extent, shards, -0.22, 0.18)
    return jnp.clip(drawn, -most, most).astype(kind)


def setup_inputs(seed: int = 0) -> dict:
    key_list = jax.random.split(jax.random.key(seed), 11)
    latents = normal_values(key_list[0], (NODES, W), 1.0, 6.0, ((0, 256),))
    upstream = normal_values(key_list[1], (NODES, W), 1.0, 6.0, ((0, 256),))
    msg_weight = normal_values(key_list[2], (LAYERS, W, W), W ** -0.5, 0.25)
    self_weight = normal_values(key_list[3], (LAYERS, W, W), W ** -0.5, 0.25)
    agg_weight = normal_values(key_list[4], (LAYERS, W, W), W ** -0.5, 0.25)
    out_weight = normal_values(key_list[5], (LAYERS, W, W), W ** -0.5, 0.25)
    gains = jnp.clip(1.0 + 0.15 * jax.random.normal(key_list[6], (LAYERS, W), jnp.float32), 0.25, 1.75)
    edge_weight = draw_edge_weight(jax.random.fold_in(key_list[10], 71), 0)
    nbr_slot = draw_nbr_slot(jax.random.fold_in(key_list[10], 71), 0)
    send_list = draw_send_list(jax.random.fold_in(key_list[10], 71), 0)
    return {"latents": latents, "upstream": upstream, "msg_weight": msg_weight, "self_weight": self_weight, "agg_weight": agg_weight, "out_weight": out_weight, "gains": gains, "edge_weight": edge_weight, "nbr_slot": nbr_slot, "send_list": send_list}


EPS = 1e-05

def silu_slope(value):
    sigma = jax.nn.sigmoid(value)
    return sigma * (1.0 + value * (1.0 - sigma))

def layer_norm(update):
    mean_value = lax.optimization_barrier(jnp.mean(update, axis=-1, keepdims=True))
    centred = update - mean_value
    inverse = lax.rsqrt(lax.optimization_barrier(jnp.mean(centred * centred, axis=-1, keepdims=True)) + EPS)
    return (centred * inverse, inverse)

def from_lower(array, axis):
    count = array.shape[axis]
    head = jnp.zeros_like(lax.slice_in_dim(array, 0, 1, axis=axis))
    return jnp.concatenate([head, lax.slice_in_dim(array, 0, count - 1, axis=axis)], axis=axis)

def from_upper(array, axis):
    count = array.shape[axis]
    tail = jnp.zeros_like(lax.slice_in_dim(array, 0, 1, axis=axis))
    return jnp.concatenate([lax.slice_in_dim(array, 1, count, axis=axis), tail], axis=axis)

def take_rows(table, ids):
    return jax.vmap(lambda part_table, part_ids: jnp.take(part_table, part_ids, axis=0))(table, ids)

def take_rows_two(table, ids):
    return jax.vmap(take_rows)(table, ids)

def extend(message, send_list):
    blocks = message.reshape(N_SPACE, N_SLAB, B_DEV, BLOCK, W)
    sent = [take_rows_two(blocks, send_list[:, :, direction, :]) for direction in range(4)]
    received = [from_lower(sent[0], 0), from_upper(sent[1], 0), from_lower(sent[2], 1), from_upper(sent[3], 1)]
    extended = jnp.concatenate([blocks] + received, axis=2)
    return extended.reshape(N_SPACE * N_SLAB, SLOTS, BLOCK, W)

def forward_layer(latent, weights, edge_weight, nbr_slot, send_list):
    msg_w, self_w, agg_w, out_w, gain_row = weights
    pre_msg = jnp.dot(latent, msg_w, preferred_element_type=jnp.float32)
    message = jax.nn.silu(pre_msg).astype(jnp.bfloat16)
    extended = extend(message, send_list)
    tiles = edge_weight.reshape(N_SPACE * N_SLAB, B_DEV, K, BLOCK, BLOCK)
    slot_ids = nbr_slot.reshape(N_SPACE * N_SLAB, B_DEV, K)
    merged_sum = jnp.zeros((N_SPACE * N_SLAB, B_DEV, BLOCK, W), jnp.float32)
    for column in range(K):
        source = take_rows(extended, slot_ids[:, :, column])
        merged_sum = merged_sum + jnp.einsum('dbij,dbjw->dbiw', tiles[:, :, column].astype(jnp.float32), source.astype(jnp.float32))
    merged = merged_sum.reshape(NODES, W).astype(jnp.bfloat16)
    pre_hidden = jnp.dot(latent, self_w, preferred_element_type=jnp.float32) + jnp.dot(merged, agg_w, preferred_element_type=jnp.float32)
    hidden = jax.nn.silu(pre_hidden).astype(jnp.bfloat16)
    update = jnp.dot(hidden, out_w, preferred_element_type=jnp.float32)
    normed, inverse = layer_norm(update)
    output = (latent.astype(jnp.float32) + gain_row * normed).astype(jnp.bfloat16)
    return (output, (latent, pre_msg, merged, pre_hidden, hidden, normed, inverse))

def backward_layer(grad_y, saved, weights, edge_weight, nbr_slot, send_list):
    latent, pre_msg, merged, pre_hidden, hidden, normed, inverse = saved
    msg_w, self_w, agg_w, out_w, gain_row = weights
    grad_gain_row = lax.optimization_barrier(jnp.sum(grad_y * normed, axis=0))
    grad_norm = grad_y * gain_row
    grad_update = inverse * (grad_norm - lax.optimization_barrier(jnp.mean(grad_norm, axis=-1, keepdims=True)) - normed * lax.optimization_barrier(jnp.mean(grad_norm * normed, axis=-1, keepdims=True)))
    grad_update = grad_update.astype(jnp.bfloat16)
    grad_out_w = jnp.dot(hidden.T, grad_update, preferred_element_type=jnp.float32)
    grad_pre_hidden = jnp.dot(grad_update, out_w.T, preferred_element_type=jnp.float32) * silu_slope(pre_hidden)
    grad_pre_hidden = grad_pre_hidden.astype(jnp.bfloat16)
    grad_self_w = jnp.dot(latent.T, grad_pre_hidden, preferred_element_type=jnp.float32)
    grad_agg_w = jnp.dot(merged.T, grad_pre_hidden, preferred_element_type=jnp.float32)
    grad_merged = jnp.dot(grad_pre_hidden, agg_w.T, preferred_element_type=jnp.float32).astype(jnp.bfloat16)
    grad_merged = grad_merged.reshape(N_SPACE * N_SLAB, B_DEV, BLOCK, W).astype(jnp.float32)
    tiles = edge_weight.reshape(N_SPACE * N_SLAB, B_DEV, K, BLOCK, BLOCK)
    slot_ids = nbr_slot.reshape(N_SPACE * N_SLAB, B_DEV, K)
    grad_extended = jnp.zeros((N_SPACE * N_SLAB, SLOTS, BLOCK, W), jnp.float32)
    for column in range(K):
        contrib = jnp.einsum('dbij,dbiw->dbjw', tiles[:, :, column].astype(jnp.float32), grad_merged)
        chooser = (slot_ids[:, :, column][:, :, None] == jnp.arange(SLOTS, dtype=jnp.int32)).astype(jnp.float32)
        grad_extended = grad_extended + jnp.einsum('dbe,dbjw->dejw', chooser, contrib)
    grad_extended = grad_extended.reshape(N_SPACE, N_SLAB, SLOTS, BLOCK, W)
    grad_message = grad_extended[:, :, :B_DEV]
    halo_grad = grad_extended[:, :, B_DEV:].astype(jnp.bfloat16).reshape(N_SPACE, N_SLAB, 4, HALO, BLOCK, W)
    returned = [from_upper(halo_grad[:, :, 0], 0), from_lower(halo_grad[:, :, 1], 0), from_upper(halo_grad[:, :, 2], 1), from_lower(halo_grad[:, :, 3], 1)]
    for direction in range(4):
        chooser = (send_list[:, :, direction, :, None] == jnp.arange(B_DEV, dtype=jnp.int32)).astype(jnp.float32)
        grad_message = grad_message + jnp.einsum('xytb,xytjw->xybjw', chooser, returned[direction].astype(jnp.float32))
    grad_pre_msg = (grad_message.reshape(NODES, W) * silu_slope(pre_msg)).astype(jnp.bfloat16)
    grad_msg_w = jnp.dot(latent.T, grad_pre_msg, preferred_element_type=jnp.float32)
    grad_x = grad_y + jnp.dot(grad_pre_hidden, self_w.T, preferred_element_type=jnp.float32) + jnp.dot(grad_pre_msg, msg_w.T, preferred_element_type=jnp.float32)
    return (grad_x, (grad_msg_w, grad_self_w, grad_agg_w, grad_out_w, grad_gain_row))

def reference(latents, upstream, msg_weight, self_weight, agg_weight, out_weight, gains, edge_weight, nbr_slot, send_list):
    latent = latents
    saved_all = []
    for layer in range(LAYERS):
        weights = (msg_weight[layer], self_weight[layer], agg_weight[layer], out_weight[layer], gains[layer])
        latent, saved = forward_layer(latent, weights, edge_weight, nbr_slot, send_list)
        saved_all.append(saved)
    grad_now = upstream.astype(jnp.float32)
    collected = [None] * LAYERS
    for layer in reversed(range(LAYERS)):
        weights = (msg_weight[layer], self_weight[layer], agg_weight[layer], out_weight[layer], gains[layer])
        grad_now, collected[layer] = backward_layer(grad_now, saved_all[layer], weights, edge_weight, nbr_slot, send_list)
    stacks = [jnp.stack([parts[index] for parts in collected]) for index in range(5)]
    return (latent, grad_now, stacks[0], stacks[1], stacks[2], stacks[3], stacks[4])
```

```python
import jax
import jax.numpy as jnp
from jax import lax
from jax.experimental import pallas as pl
from jax.experimental.pallas import tpu as pltpu
from jax.sharding import PartitionSpec as P

EPS = 1e-05
BF = jnp.bfloat16
F32 = jnp.float32
MESH = pl.DeviceIdType.MESH

W = 512
BLOCK = 128
OWN = 4
TILES = 6
SLOTS = 12
ROWS = OWN * BLOCK
COLS = SLOTS * BLOCK
LAYERS = 2
NY, NZH, NCORE = 4, 4, 2
NX, NZL = 4, 2
NZ = NZH * NZL
N_SPACE = NY * NZH * NCORE
N_SLAB = NX * NZL
SHARE = W // N_SPACE

BUNDLE_TILES = (4, 5, 1)
CHUNK = 64


def sigmoid(v):
    return 0.5 * jnp.tanh(0.5 * v) + 0.5


def dot(a, b, ca, cb):
    return lax.dot_general(a, b, (((ca,), (cb,)), ((), ())), preferred_element_type=F32)


def loop(count, body):
    def step(i, carry):
        body(i)
        return carry

    lax.fori_loop(0, count, step, 0)


def rows_of(i, size):
    return pl.ds(pl.multiple_of(i * size, size), size)


class Bundle:
    def __init__(self, refs, place):
        (self.grad, self.held, self.y1, self.y2, self.x1, self.x2, self.z, self.full,
         self.send, self.recv) = refs
        self.place = place
        self.next = 0

    def copy(self, src, dst, device):
        i = self.next
        self.next += 1
        c = pltpu.make_async_remote_copy(
            src_ref=src, dst_ref=dst, send_sem=self.send.at[i], recv_sem=self.recv.at[i],
            device_id=device, device_id_type=MESH,
        )
        c.start()
        return c

    def add(self, dst, *others):
        total = dst[...].astype(F32)
        for other in others:
            total = total + other[...].astype(F32)
        dst[...] = total.astype(BF)

    def core_start(self):
        core = self.place["core"]
        self.core_copy = self.copy(self.grad.at[1 - core], self.held, self.place["at"](core=1 - core))

    def core_done(self):
        core = self.place["core"]
        self.core_copy.wait()

        def body(i):
            a, b = i // NX, i % NX
            self.held[a, b] = (
                self.held[a, b].astype(F32) + self.grad[core, a, b].astype(F32)
            ).astype(BF)

        loop(NY * NX, body)

    def halving_start(self, axis):
        me = self.place[axis]
        self.axis = axis
        if axis == "y":
            self.view = lambda i, half: self.held.at[i, :, pl.ds(2 * half, 2)]
            self.one, self.two = self.y1, self.y2
        else:
            self.view = lambda i, half: self.held.at[self.place["y"], i, pl.ds(2 * half, 2)]
            self.one, self.two = self.x1, self.x2
        near, far, cross = me ^ 1, me ^ 3, me ^ 2
        at = self.place["at"]
        self.step_one = [
            self.copy(self.view(cross, 0), self.one.at[0, 1], at(**{axis: near})),
            self.copy(self.view(cross, 1), self.one.at[1, 1], at(**{axis: far})),
            self.copy(self.view(near, 0), self.one.at[0, 0], at(**{axis: near})),
            self.copy(self.view(far, 1), self.one.at[1, 0], at(**{axis: far})),
        ]

    def halving_middle(self):
        me = self.place[self.axis]
        near, far = me ^ 1, me ^ 3
        at = self.place["at"]
        self.step_one[0].wait()
        self.add(self.view(far, 0), self.one.at[0, 1])
        self.step_two = [self.copy(self.view(far, 0), self.two.at[0], at(**{self.axis: far}))]
        self.step_one[1].wait()
        self.add(self.view(near, 1), self.one.at[1, 1])
        self.step_two.append(self.copy(self.view(near, 1), self.two.at[1], at(**{self.axis: near})))

    def halving_done(self):
        me = self.place[self.axis]
        self.step_one[2].wait()
        self.step_one[3].wait()
        for half in range(2):
            self.step_two[half].wait()
            self.add(self.view(me, half), self.one.at[half, 0], self.two.at[half])

    def z_start(self):
        place = self.place
        z = place["zh"] * NZL + place["zl"]
        self.z_copies = []
        for j in range(1, NZ):
            there = lax.rem(z + j, NZ)
            zh, zl = there // NZL, lax.rem(there, NZL)
            self.z_copies.append(
                self.copy(self.held.at[place["y"], place["x"], zh], self.z.at[j - 1], place["at"](zh=zh, zl=zl))
            )

    def z_done(self):
        place = self.place
        total = self.held[place["y"], place["x"], place["zh"]].astype(F32)
        for j, c in enumerate(self.z_copies):
            c.wait()
            total = total + self.z[j].astype(F32)
        self.full[place["x"]] = total.astype(BF)

    def gather_start(self):
        place = self.place
        mine = self.full.at[place["x"]]
        self.gather_copies = [
            self.copy(mine, mine, place["at"](x=lax.rem(place["x"] + j, NX))) for j in range(1, NX)
        ]

    def gather_done(self):
        for c in self.gather_copies:
            c.wait()

    def matrix(self, tile):
        return [self.full[q, :, tile * 128 : (tile + 1) * 128].astype(F32) for q in range(NX)]


N_COPIES = 1 + 6 + 6 + (NZ - 1) + (NX - 1)


def bundle_scratch(tiles):
    c = tiles * 128
    return [
        pltpu.VMEM((NCORE, NY, NX, NZH, SHARE, c), BF),
        pltpu.VMEM((NY, NX, NZH, SHARE, c), BF),
        pltpu.VMEM((2, 2, NX, 2, SHARE, c), BF),
        pltpu.VMEM((2, NX, 2, SHARE, c), BF),
        pltpu.VMEM((2, 2, 2, SHARE, c), BF),
        pltpu.VMEM((2, 2, SHARE, c), BF),
        pltpu.VMEM((NZ - 1, SHARE, c), BF),
        pltpu.VMEM((NX, SHARE, c), BF),
        pltpu.SemaphoreType.DMA((N_COPIES,)),
        pltpu.SemaphoreType.DMA((N_COPIES,)),
    ]


def kernel(
    lat_in, up_in, wm_in, ws_in, wa_in, wo_in, gains, edge_in, nbr, sends,
    lat_out, grad_out, gm_out, gs_out, ga_out, go_out, gg_out,
    xs, up, wm, ws, wa, wo, edge, adj, own, ext, out_blocks, back, ret,
    pm, ph, normed, inverse, merged, hidden, acc, acc2, gy, gu, gph, gmg, gpm, in_sem, out_sem,
    halo_send, halo_recv, *bundle_refs,
):
    space = lax.axis_index("space")
    slab = lax.axis_index("slab")
    core = lax.rem(space, NCORE)
    zh = lax.rem(space // NCORE, NZH)
    y = space // (NCORE * NZH)
    zl = lax.rem(slab, NZL)
    x = slab // NZL

    def at(**new):
        p = {"core": core, "zh": zh, "y": y, "zl": zl, "x": x, **new}
        return ((p["y"] * NZH + p["zh"]) * NCORE + p["core"], p["x"] * NZL + p["zl"])

    place = {"core": core, "zh": zh, "y": y, "zl": zl, "x": x, "at": at}
    s_up, s_down = lax.rem(space + 1, N_SPACE), lax.rem(space + N_SPACE - 1, N_SPACE)
    l_up, l_down = lax.rem(slab + 1, N_SLAB), lax.rem(slab + N_SLAB - 1, N_SLAB)
    ahead = [(s_up, slab), (s_down, slab), (space, l_up), (space, l_down)]
    behind = [ahead[1], ahead[0], ahead[3], ahead[2]]

    pairs = [
        (lat_in, xs.at[0]), (wm_in, wm), (ws_in, ws), (edge_in, edge), (wa_in, wa), (wo_in, wo), (up_in, up),
    ]
    loads = [pltpu.make_async_copy(a, b, in_sem.at[i]) for i, (a, b) in enumerate(pairs)]
    for c in loads:
        c.start()
    lat_load, wm_load, ws_load, edge_load, wa_load, wo_load, up_load = loads

    barrier = pltpu.get_barrier_semaphore()
    partners = list(ahead) + [at(core=1 - core), at(y=y ^ 1), at(y=y ^ 3)]
    partners += [at(x=lax.rem(x + j, NX)) for j in range(1, NX)]
    z = zh * NZL + zl
    for j in range(1, NZ):
        there = lax.rem(z + j, NZ)
        partners.append(at(zh=there // NZL, zl=lax.rem(there, NZL)))
    for p in partners:
        pl.semaphore_signal(barrier, inc=1, device_id=p, device_id_type=MESH)

    count = len(bundle_refs) // len(BUNDLE_TILES)
    bundles = [Bundle(bundle_refs[i * count : (i + 1) * count], place) for i in range(len(BUNDLE_TILES))]

    def matmul(out, a, b, ca, cb):
        def body(i):
            r = rows_of(i, 256)
            out[r] = dot(a[r] if ca == 1 else a[:, r], b[...], ca, cb)

        loop(ROWS // 256, body)

    def matmul_add(out, a, b, ca, cb):
        def body(i):
            r = rows_of(i, 256)
            out[r] = out[r] + dot(a[r] if ca == 1 else a[:, r], b[...], ca, cb)

        loop(ROWS // 256, body)

    def halo(src, dst, peers, exchange):
        copies = []
        for d in range(4):
            c = pltpu.make_async_remote_copy(
                src_ref=src(d), dst_ref=dst(d), send_sem=halo_send.at[exchange, d],
                recv_sem=halo_recv.at[exchange, d], device_id=peers[d], device_id_type=MESH,
            )
            c.start()
            copies.append(c)
        return copies

    for l in range(LAYERS):
        if l == 0:
            lat_load.wait()
            wm_load.wait()
        matmul(pm.at[l], xs.at[l], wm.at[l], 1, 0)

        def silu_message(i, l=l):
            v = pm[l, rows_of(i, CHUNK)]
            own[l, i // 2, rows_of(lax.rem(i, 2), CHUNK)] = (v * sigmoid(v)).astype(BF)

        loop(ROWS // CHUNK, silu_message)
        for d in range(4):
            for t in range(2):
                out_blocks[l, d, t] = own[l, sends[d, t]]
        if l == 0:
            pl.semaphore_wait(barrier, len(partners))
        copies = halo(
            lambda d: out_blocks.at[l, d], lambda d: ext.at[l, d], ahead, l
        )
        if l == 0:
            edge_load.wait()

            def build(i):
                b = i // SLOTS
                e = lax.rem(i, SLOTS)
                total = jnp.zeros((BLOCK, BLOCK), F32)
                for k in range(TILES):
                    keep = jnp.where(nbr[b, k] == e, 1.0, 0.0)
                    total = total + edge[b, k].astype(F32) * keep
                adj[e, rows_of(b, BLOCK), :] = total.astype(BF)

            loop(OWN * SLOTS, build)
            ws_load.wait()

        matmul(ph.at[l], xs.at[l], ws.at[l], 1, 0)

        def adjacency(e, blocks):
            return jnp.concatenate([adj[e + j] for j in range(blocks)], axis=1)

        acc[...] = dot(adjacency(0, OWN), own[l].reshape(ROWS, W), 1, 0)
        for d in range(4):
            copies[d].wait()
            acc[...] += dot(adjacency(OWN + 2 * d, 2), ext[l, d].reshape(2 * BLOCK, W), 1, 0)
        merged[l] = acc[...].astype(BF)
        if l == 0:
            wa_load.wait()
            wo_load.wait()
        matmul_add(ph.at[l], merged.at[l], wa.at[l], 1, 0)

        def silu_hidden(i, l=l):
            r = rows_of(i, CHUNK)
            v = ph[l, r]
            hidden[l, r] = (v * sigmoid(v)).astype(BF)

        loop(ROWS // CHUNK, silu_hidden)
        matmul(acc, hidden.at[l], wo.at[l], 1, 0)

        def norm(i, l=l):
            r = rows_of(i, CHUNK)
            u = acc[r]
            centred = u - jnp.mean(u, axis=-1, keepdims=True)
            inv = lax.rsqrt(jnp.mean(centred * centred, axis=-1, keepdims=True) + EPS)
            n = centred * inv
            normed[l, r] = n
            inverse[l, r] = inv
            xs[l + 1, r] = (xs[l, r].astype(F32) + gains[l : l + 1, :] * n).astype(BF)

        loop(ROWS // CHUNK, norm)

    out_copy = pltpu.make_async_copy(xs.at[LAYERS], lat_out, out_sem.at[0])
    out_copy.start()

    def weight_grad(bundle, tile, a, g):
        for i in range(2):
            r = pl.ds(i * 256, 256)
            v = dot(a[:, r], g[...], 0, 0).astype(BF).reshape(2, NZH, NCORE, SHARE, W)
            for c in range(NCORE):
                for q in range(NX):
                    bundle.grad[c, pl.ds(2 * i, 2), q, :, :, tile * 128 : (tile + 1) * 128] = v[
                        :, :, c, :, q * 128 : (q + 1) * 128
                    ]

    def gain_grad(bundle, tile, row):
        v = jnp.transpose(jnp.broadcast_to(row, (128, W))).astype(BF).reshape(NY, NZH, NCORE, SHARE, 128)
        for c in range(NCORE):
            for q in range(NX):
                bundle.grad[c, :, q, :, :, tile * 128 : (tile + 1) * 128] = v[:, :, c]

    for l in reversed(range(LAYERS)):
        if l == LAYERS - 1:
            up_load.wait()

            def start(i):
                r = rows_of(i, CHUNK)
                gy[r] = up[r].astype(F32)

            loop(ROWS // CHUNK, start)

        def norm_grad(i, row, l=l):
            r = rows_of(i, CHUNK)
            g = gy[r]
            n = normed[l, r]
            row = row + jnp.sum(g * n, axis=0, keepdims=True)
            g = g * gains[l : l + 1, :]
            u = g - jnp.mean(g, axis=-1, keepdims=True) - n * jnp.mean(g * n, axis=-1, keepdims=True)
            gu[r] = (inverse[l, r] * u).astype(BF)
            return row

        gain_row = lax.fori_loop(0, ROWS // CHUNK, norm_grad, jnp.zeros((1, W), F32))
        matmul(acc, gu, wo.at[l], 1, 1)

        def hidden_grad(i, l=l):
            r = rows_of(i, CHUNK)
            v = ph[l, r]
            s = sigmoid(v)
            gph[l, r] = (acc[r] * (s * (1.0 + v * (1.0 - s)))).astype(BF)

        loop(ROWS // CHUNK, hidden_grad)
        matmul(acc, gph.at[l], wa.at[l], 1, 1)
        gmg[...] = acc[...].astype(BF)
        for e in range(OWN, SLOTS):
            back[l, (e - OWN) // 2, (e - OWN) % 2] = dot(adj[e], gmg[...], 0, 0).astype(BF)
        copies = halo(lambda d: back.at[l, d], lambda d: ret.at[l, d], behind, LAYERS + l)

        bundle = bundles[LAYERS - 1 - l]
        t = 0
        if l == 0:
            weight_grad(bundle, 0, xs.at[1], gpm)
            t = 1
        weight_grad(bundle, t, hidden.at[l], gu)
        weight_grad(bundle, t + 1, xs.at[l], gph.at[l])
        weight_grad(bundle, t + 2, merged.at[l], gph.at[l])
        gain_grad(bundle, t + 3, gain_row)
        bundle.core_start()
        for e in range(OWN):
            acc2[e * BLOCK : (e + 1) * BLOCK] = dot(adj[e], gmg[...], 0, 0)
        matmul_add(gy, gph.at[l], ws.at[l], 1, 1)
        bundle.core_done()
        bundle.halving_start("y")
        bundle.halving_middle()
        bundle.halving_done()
        bundle.halving_start("x")
        bundle.halving_middle()
        bundle.halving_done()
        bundle.z_start()
        for c in copies:
            c.wait()

        def message_grad(i, l=l):
            b = i // 2
            r = rows_of(i, CHUNK)
            inner = rows_of(lax.rem(i, 2), CHUNK)
            total = acc2[r]
            for d in range(4):
                for t in range(2):
                    keep = jnp.where(sends[d, t] == b, 1.0, 0.0)
                    total = total + ret[l, d, t, inner].astype(F32) * keep
            v = pm[l, r]
            s = sigmoid(v)
            gpm[r] = (total * (s * (1.0 + v * (1.0 - s)))).astype(BF)

        loop(ROWS // CHUNK, message_grad)
        if l == 0:
            weight_grad(bundles[2], 0, xs.at[0], gpm)
            bundles[2].core_start()
        matmul_add(gy, gpm, wm.at[l], 1, 1)

    grad_copy = pltpu.make_async_copy(gy, grad_out, out_sem.at[1])
    grad_copy.start()
    tail = bundles[2]
    tail.core_done()
    tail.halving_start("y")
    for bundle in bundles[:2]:
        bundle.z_done()
        bundle.gather_start()
    tail.halving_middle()
    tail.halving_done()
    tail.halving_start("x")
    tail.halving_middle()
    tail.halving_done()
    tail.z_start()
    for bundle in bundles[:2]:
        bundle.gather_done()
    tail.z_done()
    tail.gather_start()

    def put(out, l, bundle, tile):
        for q, v in enumerate(bundle.matrix(tile)):
            out[l, :, q * 128 : (q + 1) * 128] = v

    def put_gain(l, bundle, tile):
        v = bundle.matrix(tile)[0]
        same = lax.broadcasted_iota(jnp.int32, v.shape, 0) == lax.broadcasted_iota(jnp.int32, v.shape, 1)
        gg_out[l : l + 1, :] = jnp.sum(jnp.where(same, v, 0.0), axis=0, keepdims=True)[:, :SHARE]

    put(go_out, 1, bundles[0], 0)
    put(gs_out, 1, bundles[0], 1)
    put(ga_out, 1, bundles[0], 2)
    put_gain(1, bundles[0], 3)
    put(gm_out, 1, bundles[1], 0)
    put(go_out, 0, bundles[1], 1)
    put(gs_out, 0, bundles[1], 2)
    put(ga_out, 0, bundles[1], 3)
    put_gain(0, bundles[1], 4)
    tail.gather_done()
    put(gm_out, 0, tail, 0)
    out_copy.wait()
    grad_copy.wait()


def local(
    latents, upstream, msg_weight, self_weight, agg_weight, out_weight, gains, edge_weight, nbr_slot, send_list
):
    sends = send_list.reshape(4, send_list.shape[-1])
    hbm = pl.BlockSpec(memory_space=pl.ANY)
    vmem = pl.BlockSpec(memory_space=pltpu.VMEM)
    smem = pl.BlockSpec(memory_space=pltpu.SMEM)
    share = jax.ShapeDtypeStruct((LAYERS, SHARE, W), F32)
    scratch = [
        pltpu.VMEM((LAYERS + 1, ROWS, W), BF),
        pltpu.VMEM((ROWS, W), BF),
        pltpu.VMEM((LAYERS, W, W), BF),
        pltpu.VMEM((LAYERS, W, W), BF),
        pltpu.VMEM((LAYERS, W, W), BF),
        pltpu.VMEM((LAYERS, W, W), BF),
        pltpu.VMEM((OWN, TILES, BLOCK, BLOCK), BF),
        pltpu.VMEM((SLOTS, ROWS, BLOCK), BF),
        pltpu.VMEM((LAYERS, OWN, BLOCK, W), BF),
        pltpu.VMEM((LAYERS, 4, 2, BLOCK, W), BF),
        pltpu.VMEM((LAYERS, 4, 2, BLOCK, W), BF),
        pltpu.VMEM((LAYERS, 4, 2, BLOCK, W), BF),
        pltpu.VMEM((LAYERS, 4, 2, BLOCK, W), BF),
        pltpu.VMEM((LAYERS, ROWS, W), F32),
        pltpu.VMEM((LAYERS, ROWS, W), F32),
        pltpu.VMEM((LAYERS, ROWS, W), F32),
        pltpu.VMEM((LAYERS, ROWS, 1), F32),
        pltpu.VMEM((LAYERS, ROWS, W), BF),
        pltpu.VMEM((LAYERS, ROWS, W), BF),
        pltpu.VMEM((ROWS, W), F32),
        pltpu.VMEM((ROWS, W), F32),
        pltpu.VMEM((ROWS, W), F32),
        pltpu.VMEM((ROWS, W), BF),
        pltpu.VMEM((LAYERS, ROWS, W), BF),
        pltpu.VMEM((ROWS, W), BF),
        pltpu.VMEM((ROWS, W), BF),
        pltpu.SemaphoreType.DMA((7,)),
        pltpu.SemaphoreType.DMA((2,)),
        pltpu.SemaphoreType.DMA((2 * LAYERS, 4)),
        pltpu.SemaphoreType.DMA((2 * LAYERS, 4)),
    ]
    for tiles in BUNDLE_TILES:
        scratch += bundle_scratch(tiles)
    out = pl.pallas_call(
        kernel,
        out_shape=(
            jax.ShapeDtypeStruct((ROWS, W), BF),
            jax.ShapeDtypeStruct((ROWS, W), F32),
            share, share, share, share,
            jax.ShapeDtypeStruct((LAYERS, SHARE), F32),
        ),
        in_specs=[hbm, hbm, hbm, hbm, hbm, hbm, vmem, hbm, smem, smem],
        out_specs=(hbm, hbm, vmem, vmem, vmem, vmem, vmem),
        scratch_shapes=scratch,
        compiler_params=pltpu.CompilerParams(
            collective_id=0, has_side_effects=True, vmem_limit_bytes=60 * 1024 * 1024
        ),
        cost_estimate=pl.CostEstimate(flops=10 * 10**9, bytes_accessed=10 * 2**20, transcendentals=2 * 10**6),
    )(latents, upstream, msg_weight, self_weight, agg_weight, out_weight, gains, edge_weight, nbr_slot, sends)
    return out


def solution(mesh):
    rows = P(("space", "slab"), None)
    return jax.shard_map(
        local,
        mesh=mesh,
        in_specs=(
            rows, rows, P(), P(), P(), P(), P(),
            P(("space", "slab"), None, None, None), rows, P("space", "slab", None, None),
        ),
        out_specs=(
            rows, rows, P(None, "space", None), P(None, "space", None), P(None, "space", None),
            P(None, "space", None), P(None, "space"),
        ),
        check_vma=False,
    )
```

```python
import jax
import jax.numpy as jnp
from jax import lax
from jax.experimental import pallas as pl
from jax.experimental.pallas import tpu as pltpu
from jax.sharding import PartitionSpec as P

EPS = 1e-05
BF = jnp.bfloat16
F32 = jnp.float32
MESH = pl.DeviceIdType.MESH

W = 512
BLOCK = 128
OWN = 4
TILES = 6
SLOTS = 12
ROWS = OWN * BLOCK
COLS = SLOTS * BLOCK
LAYERS = 2
NY, NZH, NCORE = 4, 4, 2
NX, NZL = 4, 2
NZ = NZH * NZL
N_SPACE = NY * NZH * NCORE
N_SLAB = NX * NZL
SHARE = W // N_SPACE

BUNDLE_TILES = (4, 5, 1)
PARTS = NZH


def sigmoid(v):
    return 0.5 * jnp.tanh(0.5 * v) + 0.5


def slope(v, s):
    return s * (1.0 + v * (1.0 - s))


def dot(a, b, ca, cb):
    return lax.dot_general(a, b, (((ca,), (cb,)), ((), ())), preferred_element_type=F32)


def loop(count, body):
    def step(i, carry):
        body(i)
        return carry

    lax.fori_loop(0, count, step, 0)


def rows_of(i, size):
    return pl.ds(pl.multiple_of(i * size, size), size)


def block_rows(b):
    return slice(b * BLOCK, (b + 1) * BLOCK)


def add(dst, *others):
    total = dst[...].astype(F32)
    for other in others:
        total = total + other[...].astype(F32)
    dst[...] = total.astype(BF)


class Bundle:
    def __init__(self, refs, place):
        self.grad, self.held, self.z, self.full, self.send, self.recv, *self.more = refs
        self.place = place
        self.next = 0

    def copy(self, src, dst, device):
        i = self.next
        self.next += 1
        c = pltpu.make_async_remote_copy(
            src_ref=src, dst_ref=dst, send_sem=self.send.at[i], recv_sem=self.recv.at[i],
            device_id=device, device_id_type=MESH,
        )
        c.start()
        return c

    def core_start(self):
        core = self.place["core"]
        self.core_copy = self.copy(self.grad.at[1 - core], self.held, self.place["at"](core=1 - core))

    def core_done(self):
        core = self.place["core"]
        self.core_copy.wait()

        def body(i):
            self.held[i] = (self.held[i].astype(F32) + self.grad[core, i].astype(F32)).astype(BF)

        loop(NY, body)

    def z_start(self):
        place = self.place
        z = place["zh"] * NZL + place["zl"]
        self.z_copies = []
        for j in range(1, NZ):
            there = lax.rem(z + j, NZ)
            zh, zl = there // NZL, lax.rem(there, NZL)
            self.z_copies.append(
                self.copy(self.held.at[place["y"], place["x"], zh], self.z.at[j - 1], place["at"](zh=zh, zl=zl))
            )

    def z_done(self):
        place = self.place
        total = self.held[place["y"], place["x"], place["zh"]].astype(F32)
        for j, c in enumerate(self.z_copies):
            c.wait()
            total = total + self.z[j].astype(F32)
        self.full[place["x"]] = total.astype(BF)

    def gather_start(self):
        place = self.place
        mine = self.full.at[place["x"]]
        self.gather_copies = [
            self.copy(mine, mine, place["at"](x=lax.rem(place["x"] + j, NX))) for j in range(1, NX)
        ]

    def gather_done(self):
        for c in self.gather_copies:
            c.wait()

    def matrix(self, tile):
        return [self.full[q, :, tile * 128 : (tile + 1) * 128].astype(F32) for q in range(NX)]


class Halving(Bundle):
    def setup(self):
        self.first = []
        self.second = []
        for p in range(PARTS):
            axes = ("y", "x") if p < PARTS // 2 else ("x", "y")
            near, far = (1, 3) if p % 2 == 0 else (3, 1)
            self.first.append((axes[0], near, far))
            self.second.append((axes[1], near, far))

    def view(self, p, stage, i):
        axis = (self.first if stage == 0 else self.second)[p][0]
        y, x = self.place["y"], self.place["x"]
        if stage == 0:
            return self.held.at[i, :, p] if axis == "y" else self.held.at[:, i, p]
        return self.held.at[i, x, p] if axis == "y" else self.held.at[y, i, p]

    def pairs_start(self, stage):
        self.setup()
        land = self.more[2 * stage]
        at = self.place["at"]
        self.cross, self.near, self.far = [], [], []
        for slot in (1, 0):
            for p, (axis, near, _) in enumerate((self.first, self.second)[stage]):
                me = self.place[axis]
                chunk = me ^ 2 if slot else me ^ near
                c = self.copy(self.view(p, stage, chunk), land.at[p, slot], at(**{axis: me ^ near}))
                (self.cross if slot else self.near).append(c)

    def pairs_middle(self, stage):
        land, land_two = self.more[2 * stage], self.more[2 * stage + 1]
        at = self.place["at"]
        for p, (axis, near, far) in enumerate((self.first, self.second)[stage]):
            me = self.place[axis]
            self.cross[p].wait()
            chunk = self.view(p, stage, me ^ far)
            add(chunk, land.at[p, 1])
            self.far.append(self.copy(chunk, land_two.at[p], at(**{axis: me ^ far})))

    def pairs_done(self, stage):
        land, land_two = self.more[2 * stage], self.more[2 * stage + 1]
        for p, (axis, near, far) in enumerate((self.first, self.second)[stage]):
            self.near[p].wait()
            self.far[p].wait()
            add(self.view(p, stage, self.place[axis]), land.at[p, 0], land_two.at[p])


class Direct(Bundle):
    def plane_start(self):
        place = self.place
        (land,) = self.more
        self.plane = []
        for i in range(NY):
            for j in range(NX):
                if i or j:
                    y, x = lax.rem(place["y"] + i, NY), lax.rem(place["x"] + j, NX)
                    self.plane.append(
                        self.copy(self.held.at[y, x], land.at[len(self.plane)], place["at"](y=y, x=x))
                    )

    def plane_done(self):
        (land,) = self.more
        y, x = self.place["y"], self.place["x"]
        for c in self.plane:
            c.wait()
        total = self.held[y, x].astype(F32)
        for j in range(NY * NX - 1):
            total = total + land[j].astype(F32)
        self.held[y, x] = total.astype(BF)


def bundle_scratch(tiles, direct):
    c = tiles * 128
    copies = 1 + (NZ - 1) + (NX - 1) + (NY * NX - 1 if direct else 6 * PARTS)
    refs = [
        pltpu.VMEM((NCORE, NY, NX, NZH, SHARE, c), BF),
        pltpu.VMEM((NY, NX, NZH, SHARE, c), BF),
        pltpu.VMEM((NZ - 1, SHARE, c), BF),
        pltpu.VMEM((NX, SHARE, c), BF),
        pltpu.SemaphoreType.DMA((copies,)),
        pltpu.SemaphoreType.DMA((copies,)),
    ]
    if direct:
        return refs + [pltpu.VMEM((NY * NX - 1, NZH, SHARE, c), BF)]
    return refs + [
        pltpu.VMEM((PARTS, 2, 4, SHARE, c), BF),
        pltpu.VMEM((PARTS, 4, SHARE, c), BF),
        pltpu.VMEM((PARTS, 2, SHARE, c), BF),
        pltpu.VMEM((PARTS, SHARE, c), BF),
    ]


def kernel(
    lat_in, up_in, wm_in, ws_in, wa_in, wo_in, gains_in, edge_in, nbr_in, sends_in,
    lat_out, grad_out, gm_out, gs_out, ga_out, go_out, gg_out,
    xs, up, wm, ws, wa, wo, gains, edge, nbr, sends, adj, own, ext, out_blocks, back, ret0, ret1,
    pm, ph, normed, inverse, merged, hidden, acc, acc2, gy, gu, gph, gmg, gpm, in_sem, out_sem,
    halo_send, halo_recv, *bundle_refs,
):
    space = lax.axis_index("space")
    slab = lax.axis_index("slab")
    core = lax.rem(space, NCORE)
    zh = lax.rem(space // NCORE, NZH)
    y = space // (NCORE * NZH)
    zl = lax.rem(slab, NZL)
    x = slab // NZL

    def at(**new):
        p = {"core": core, "zh": zh, "y": y, "zl": zl, "x": x, **new}
        return ((p["y"] * NZH + p["zh"]) * NCORE + p["core"], p["x"] * NZL + p["zl"])

    place = {"core": core, "zh": zh, "y": y, "zl": zl, "x": x, "at": at}
    s_up, s_down = lax.rem(space + 1, N_SPACE), lax.rem(space + N_SPACE - 1, N_SPACE)
    l_up, l_down = lax.rem(slab + 1, N_SLAB), lax.rem(slab + N_SLAB - 1, N_SLAB)
    ahead = [(s_up, slab), (s_down, slab), (space, l_up), (space, l_down)]
    behind = [ahead[1], ahead[0], ahead[3], ahead[2]]

    barrier = pltpu.get_barrier_semaphore()
    partners = list(ahead) + [at(core=1 - core)]
    partners += [at(y=lax.rem(y + i, NY), x=lax.rem(x + j, NX)) for i in range(NY) for j in range(NX) if i or j]
    z = zh * NZL + zl
    for j in range(1, NZ):
        there = lax.rem(z + j, NZ)
        partners.append(at(zh=there // NZL, zl=lax.rem(there, NZL)))
    for p in partners:
        pl.semaphore_signal(barrier, inc=1, device_id=p, device_id_type=MESH)

    pairs = [
        (lat_in, xs.at[0]), (wm_in, wm), (sends_in.at[0, 0], sends), (nbr_in, nbr), (edge_in, edge), (ws_in, ws),
        (wa_in, wa), (wo_in, wo), (gains_in, gains), (up_in, up),
    ]
    loads = [pltpu.make_async_copy(a, b, in_sem.at[i]) for i, (a, b) in enumerate(pairs)]
    for c in loads:
        c.start()
    lat_load, wm_load, sends_load, nbr_load, edge_load, ws_load, wa_load, wo_load, gains_load, up_load = loads

    count = len(bundle_scratch(1, False))
    early = Halving(bundle_refs[:count], place)
    late = Halving(bundle_refs[count : 2 * count], place)
    tail = Direct(bundle_refs[2 * count :], place)
    ret = (ret0, ret1)

    def halo(src, dst, peers, exchange, before):
        copies = []
        for d in range(4):
            before(d)
            c = pltpu.make_async_remote_copy(
                src_ref=src(d), dst_ref=dst(d), send_sem=halo_send.at[exchange, d],
                recv_sem=halo_recv.at[exchange, d], device_id=peers[d], device_id_type=MESH,
            )
            c.start()
            copies.append(c)
        return copies

    def adjacency(e, blocks, rows=slice(None)):
        return jnp.concatenate([adj[e + j, rows] for j in range(blocks)], axis=1)

    def message(l, b, latent):
        v = dot(latent, wm[l], 1, 0)
        pm[l, block_rows(b)] = v
        own[l, b] = (v * sigmoid(v)).astype(BF)

    def gathered(l):
        def pick(d):
            for t in range(2):
                out_blocks[l, d, t] = own[l, sends[t, d]]

        return pick

    lat_load.wait()
    wm_load.wait()
    for b in range(OWN):
        message(0, b, xs[0, block_rows(b)])
    sends_load.wait()
    pl.semaphore_wait(barrier, len(partners))
    gain_row = jnp.zeros((1, W), F32)

    def update_grad(l, b, g, n, inv):
        r = block_rows(b)
        row = jnp.sum(g * n, axis=0, keepdims=True)
        g = g * gains[l : l + 1, :]
        u = g - jnp.mean(g, axis=-1, keepdims=True) - n * jnp.mean(g * n, axis=-1, keepdims=True)
        u = (inv * u).astype(BF)
        gu[l, r] = u
        h = (dot(u, wo[l], 1, 1) * ph[l, r]).astype(BF)
        gph[l, r] = h
        gmg[r] = dot(h, wa[l], 1, 1).astype(BF)
        return row

    for l in range(LAYERS):
        copies = halo(lambda d: out_blocks.at[l, d], lambda d: ext.at[l, d], ahead, l, gathered(l))
        if l == 0:
            edge_load.wait()
            nbr_load.wait()

            def build(i):
                b = i // SLOTS
                e = lax.rem(i, SLOTS)
                total = jnp.zeros((BLOCK, BLOCK), F32)
                for k in range(TILES):
                    keep = jnp.where(nbr[b, k] == e, 1.0, 0.0)
                    total = total + edge[b, k].astype(F32) * keep
                adj[e, rows_of(b, BLOCK), :] = total.astype(BF)

            loop(OWN * SLOTS, build)
            for c in (ws_load, wa_load, wo_load, gains_load, up_load):
                c.wait()
        for b in range(OWN):
            r = block_rows(b)
            ph[l, r] = dot(xs[l, r], ws[l], 1, 0)
            acc[r] = dot(adjacency(0, OWN, r), own[l].reshape(ROWS, W), 1, 0)
            v = pm[l, r]
            pm[l, r] = slope(v, sigmoid(v))
        for d in range(4):
            copies[d].wait()
            if d < 3:
                for b in range(OWN):
                    r = block_rows(b)
                    acc[r] += dot(adjacency(OWN + 2 * d, 2, r), ext[l, d].reshape(2 * BLOCK, W), 1, 0)
        for b in range(OWN):
            r = block_rows(b)
            m = (acc[r] + dot(adjacency(OWN + 6, 2, r), ext[l, 3].reshape(2 * BLOCK, W), 1, 0)).astype(BF)
            merged[l, r] = m
            v = ph[l, r] + dot(m, wa[l], 1, 0)
            s = sigmoid(v)
            h = (v * s).astype(BF)
            hidden[l, r] = h
            ph[l, r] = slope(v, s)
            u = dot(h, wo[l], 1, 0)
            centred = u - jnp.mean(u, axis=-1, keepdims=True)
            inv = lax.rsqrt(jnp.mean(centred * centred, axis=-1, keepdims=True) + EPS)
            n = centred * inv
            out = (xs[l, r].astype(F32) + gains[l : l + 1, :] * n).astype(BF)
            xs[l + 1, r] = out
            if l + 1 < LAYERS:
                normed[l, r] = n
                inverse[l, r] = inv
                message(l + 1, b, out)
            else:
                gain_row = gain_row + update_grad(l, b, up[r].astype(F32), n, inv)

    def weight_grad(bundle, tile, a, g):
        for i in range(2):
            r = pl.ds(i * 256, 256)
            v = dot(a[:, r], g[...], 0, 0).astype(BF).reshape(2, NZH, NCORE, SHARE, W)
            for c in range(NCORE):
                for q in range(NX):
                    bundle.grad[c, pl.ds(2 * i, 2), q, :, :, tile * 128 : (tile + 1) * 128] = v[
                        :, :, c, :, q * 128 : (q + 1) * 128
                    ]

    def gain_grad(bundle, tile, row):
        v = jnp.transpose(jnp.broadcast_to(row, (128, W))).astype(BF).reshape(NY, NZH, NCORE, SHARE, 128)
        for c in range(NCORE):
            for q in range(NX):
                bundle.grad[c, :, q, :, :, tile * 128 : (tile + 1) * 128] = v[:, :, c]

    for l in reversed(range(LAYERS)):

        def back_grad(d, l=l):
            v = dot(adjacency(OWN + 2 * d, 2), gmg[...], 0, 0)
            back[l, d] = v.astype(BF).reshape(2, BLOCK, W)

        copies = halo(lambda d: back.at[l, d], lambda d: ret[l].at[d, pl.ds(0, 2)], behind, LAYERS + l, back_grad)

        bundle = (late, early)[l]
        t = 0
        if l == 0:
            weight_grad(bundle, 0, xs.at[1], gpm.at[1])
            t = 1
        weight_grad(bundle, t, hidden.at[l], gu.at[l])
        weight_grad(bundle, t + 1, xs.at[l], gph.at[l])
        weight_grad(bundle, t + 2, merged.at[l], gph.at[l])
        gain_grad(bundle, t + 3, gain_row)
        bundle.core_start()
        for d in range(4):
            ret[l][d, 2] = jnp.zeros((BLOCK, W), BF)
        for b in range(OWN):
            r = block_rows(b)
            acc2[r] = dot(adj[b], gmg[...], 0, 0)
            before = up[r].astype(F32) if l == LAYERS - 1 else gy[r]
            gy[r] = before + dot(gph[l, r], ws[l], 1, 1)
        if l == 0:
            early.pairs_done(1)
        bundle.core_done()
        bundle.pairs_start(0)
        bundle.pairs_middle(0)
        bundle.pairs_done(0)
        bundle.pairs_start(1)
        if l == 1:
            bundle.pairs_middle(1)
        for c in copies:
            c.wait()

        def message_grad(b, l=l):
            r = block_rows(b)
            total = acc2[r]
            for d in range(4):
                which = jnp.where(sends[0, d] == b, 0, jnp.where(sends[1, d] == b, 1, 2))
                total = total + ret[l][d, which].astype(F32)
            g = (total * pm[l, r]).astype(BF)
            gpm[l, r] = g
            return g

        if l > 0:
            gain_row = jnp.zeros((1, W), F32)
            for b in range(OWN):
                r = block_rows(b)
                g = gy[r] + dot(message_grad(b), wm[l], 1, 1)
                gy[r] = g
                gain_row = gain_row + update_grad(l - 1, b, g, normed[l - 1, r], inverse[l - 1, r])
        else:
            for b in range(OWN):
                message_grad(b)

    weight_grad(tail, 0, xs.at[0], gpm.at[0])
    tail.core_start()
    early.z_start()
    for b in range(OWN):
        r = block_rows(b)
        gy[r] += dot(gpm[0, r], wm[0], 1, 1)
    grad_copy = pltpu.make_async_copy(gy, grad_out, out_sem.at[1])
    grad_copy.start()
    out_copy = pltpu.make_async_copy(xs.at[LAYERS], lat_out, out_sem.at[0])
    out_copy.start()
    tail.core_done()
    tail.plane_start()
    late.pairs_middle(1)
    late.pairs_done(1)
    early.z_done()
    early.gather_start()
    late.z_start()
    tail.plane_done()
    tail.z_start()
    early.gather_done()

    def put(out, l, bundle, tile):
        for q, v in enumerate(bundle.matrix(tile)):
            out[l, :, q * 128 : (q + 1) * 128] = v

    def put_gain(l, bundle, tile):
        v = bundle.matrix(tile)[0]
        same = lax.broadcasted_iota(jnp.int32, v.shape, 0) == lax.broadcasted_iota(jnp.int32, v.shape, 1)
        gg_out[l : l + 1, :] = jnp.sum(jnp.where(same, v, 0.0), axis=0, keepdims=True)[:, :SHARE]

    put(go_out, 1, early, 0)
    put(gs_out, 1, early, 1)
    put(ga_out, 1, early, 2)
    put_gain(1, early, 3)
    late.z_done()
    late.gather_start()
    tail.z_done()
    tail.gather_start()
    late.gather_done()
    put(gm_out, 1, late, 0)
    put(go_out, 0, late, 1)
    put(gs_out, 0, late, 2)
    put(ga_out, 0, late, 3)
    put_gain(0, late, 4)
    tail.gather_done()
    put(gm_out, 0, tail, 0)
    out_copy.wait()
    grad_copy.wait()


PIECES = (2, 4, 1, 1, 1, 1, 1)


def hand_over(*refs):
    count = len(PIECES)
    into, out, held = refs[:count], refs[count : 2 * count], refs[2 * count : 3 * count]
    in_sem, out_sem = refs[3 * count :]
    steps = []
    for i, pieces in enumerate(PIECES):
        size = into[i].shape[0] // pieces
        for j in range(pieces):
            piece = pl.ds(j * size, size)
            n = len(steps)
            steps.append((
                pltpu.make_async_copy(into[i].at[piece], held[i].at[piece], in_sem.at[n]),
                pltpu.make_async_copy(held[i].at[piece], out[i].at[piece], out_sem.at[n]),
            ))
    for first, _ in steps:
        first.start()
    for first, second in steps:
        first.wait()
        second.start()
    for _, second in steps:
        second.wait()


def local(
    latents, upstream, msg_weight, self_weight, agg_weight, out_weight, gains, edge_weight, nbr_slot, send_list
):
    hbm = pl.BlockSpec(memory_space=pl.ANY)
    vmem = pl.BlockSpec(memory_space=pltpu.VMEM)
    share = jax.ShapeDtypeStruct((LAYERS, SHARE, W), F32)
    scratch = [
        pltpu.VMEM((LAYERS + 1, ROWS, W), BF),
        pltpu.VMEM((ROWS, W), BF),
        pltpu.VMEM((LAYERS, W, W), BF),
        pltpu.VMEM((LAYERS, W, W), BF),
        pltpu.VMEM((LAYERS, W, W), BF),
        pltpu.VMEM((LAYERS, W, W), BF),
        pltpu.VMEM((LAYERS, W), F32),
        pltpu.VMEM((OWN, TILES, BLOCK, BLOCK), BF),
        pltpu.SMEM((OWN, TILES), jnp.int32),
        pltpu.SMEM((2, 4), jnp.int32),
        pltpu.VMEM((SLOTS, ROWS, BLOCK), BF),
        pltpu.VMEM((LAYERS, OWN, BLOCK, W), BF),
        pltpu.VMEM((LAYERS, 4, 2, BLOCK, W), BF),
        pltpu.VMEM((LAYERS, 4, 2, BLOCK, W), BF),
        pltpu.VMEM((LAYERS, 4, 2, BLOCK, W), BF),
        pltpu.VMEM((4, 3, BLOCK, W), BF),
        pltpu.VMEM((4, 3, BLOCK, W), BF),
        pltpu.VMEM((LAYERS, ROWS, W), F32),
        pltpu.VMEM((LAYERS, ROWS, W), F32),
        pltpu.VMEM((LAYERS, ROWS, W), F32),
        pltpu.VMEM((LAYERS, ROWS, 1), F32),
        pltpu.VMEM((LAYERS, ROWS, W), BF),
        pltpu.VMEM((LAYERS, ROWS, W), BF),
        pltpu.VMEM((ROWS, W), F32),
        pltpu.VMEM((ROWS, W), F32),
        pltpu.VMEM((ROWS, W), F32),
        pltpu.VMEM((LAYERS, ROWS, W), BF),
        pltpu.VMEM((LAYERS, ROWS, W), BF),
        pltpu.VMEM((ROWS, W), BF),
        pltpu.VMEM((LAYERS, ROWS, W), BF),
        pltpu.SemaphoreType.DMA((10,)),
        pltpu.SemaphoreType.DMA((2,)),
        pltpu.SemaphoreType.DMA((2 * LAYERS, 4)),
        pltpu.SemaphoreType.DMA((2 * LAYERS, 4)),
    ]
    for i, tiles in enumerate(BUNDLE_TILES):
        scratch += bundle_scratch(tiles, i == 2)
    shapes = (
        jax.ShapeDtypeStruct((ROWS, W), BF),
        jax.ShapeDtypeStruct((ROWS, W), F32),
        share, share, share, share,
        jax.ShapeDtypeStruct((LAYERS, SHARE), F32),
    )
    out = pl.pallas_call(
        kernel,
        out_shape=shapes,
        in_specs=[hbm] * 10,
        out_specs=(hbm, hbm, vmem, vmem, vmem, vmem, vmem),
        scratch_shapes=scratch,
        compiler_params=pltpu.CompilerParams(
            collective_id=0, has_side_effects=True, vmem_limit_bytes=60 * 1024 * 1024
        ),
        cost_estimate=pl.CostEstimate(flops=10 * 10**9, bytes_accessed=10 * 2**20, transcendentals=2 * 10**6),
    )(latents, upstream, msg_weight, self_weight, agg_weight, out_weight, gains, edge_weight, nbr_slot, jnp.swapaxes(send_list, 2, 3))
    return pl.pallas_call(
        hand_over,
        out_shape=shapes,
        in_specs=[hbm] * 7,
        out_specs=[hbm] * 7,
        scratch_shapes=[pltpu.VMEM(v.shape, v.dtype) for v in shapes]
        + [pltpu.SemaphoreType.DMA((sum(PIECES),)), pltpu.SemaphoreType.DMA((sum(PIECES),))],
    )(*out)


def solution(mesh):
    rows = P(("space", "slab"), None)
    return jax.shard_map(
        local,
        mesh=mesh,
        in_specs=(
            rows, rows, P(), P(), P(), P(), P(),
            P(("space", "slab"), None, None, None), rows, P("space", "slab", None, None),
        ),
        out_specs=(
            rows, rows, P(None, "space", None), P(None, "space", None), P(None, "space", None),
            P(None, "space", None), P(None, "space"),
        ),
        check_vma=False,
    )
```

```python
import jax
import jax.numpy as jnp
from jax import lax
from jax.experimental import pallas as pl
from jax.experimental.pallas import tpu as pltpu
from jax.sharding import PartitionSpec as P

EPS = 1e-05
BF = jnp.bfloat16
F32 = jnp.float32
MESH = pl.DeviceIdType.MESH

W = 512
BLOCK = 128
OWN = 4
TILES = 6
SLOTS = 12
ROWS = OWN * BLOCK
COLS = SLOTS * BLOCK
LAYERS = 2
NY, NZH, NCORE = 4, 4, 2
NX, NZL = 4, 2
NZ = NZH * NZL
N_SPACE = NY * NZH * NCORE
N_SLAB = NX * NZL
SHARE = W // N_SPACE

BUNDLE_TILES = (2, 2)
ORDER = (2, 3, 0, 1)
ORDER_IN = (0, 1, 2, 3)
HALF = NZH // 2
HALO_ROWS = 2 * BLOCK


def sigmoid(v):
    return 0.5 * jnp.tanh(0.5 * v) + 0.5


def slope(v, s):
    return s * (1.0 + v * (1.0 - s))


def dot(a, b, ca, cb):
    return lax.dot_general(a, b, (((ca,), (cb,)), ((), ())), preferred_element_type=F32)


def loop(count, body):
    def step(i, carry):
        body(i)
        return carry

    lax.fori_loop(0, count, step, 0)


def rows_of(i, size):
    return pl.ds(pl.multiple_of(i * size, size), size)


def block_rows(b):
    return slice(b * BLOCK, (b + 1) * BLOCK)


def add(dst, *others):
    total = dst[...].astype(F32)
    for other in others:
        total = total + other[...].astype(F32)
    dst[...] = total.astype(BF)


class Bundle:
    def __init__(self, refs, place):
        self.grad, self.held, self.z, self.full, self.send, self.recv, *self.land = refs
        self.place = place
        self.next = 0

    def copy(self, src, dst, device):
        i = self.next
        self.next += 1
        c = pltpu.make_async_remote_copy(
            src_ref=src, dst_ref=dst, send_sem=self.send.at[i], recv_sem=self.recv.at[i],
            device_id=device, device_id_type=MESH,
        )
        c.start()
        return c

    def core_start(self):
        core = self.place["core"]
        self.core_copy = self.copy(self.grad.at[1 - core], self.held, self.place["at"](core=1 - core))

    def core_done(self):
        core = self.place["core"]
        self.core_copy.wait()

        def body(i):
            self.held[i] = (self.held[i].astype(F32) + self.grad[core, i].astype(F32)).astype(BF)

        loop(NY, body)

    def z_start(self):
        place = self.place
        z = place["zh"] * NZL + place["zl"]
        self.z_copies = []
        for j in range(1, NZ):
            there = lax.rem(z + j, NZ)
            zh, zl = there // NZL, lax.rem(there, NZL)
            self.z_copies.append(
                self.copy(self.held.at[place["y"], place["x"], zh], self.z.at[j - 1], place["at"](zh=zh, zl=zl))
            )

    def z_done(self):
        place = self.place
        total = self.held[place["y"], place["x"], place["zh"]].astype(F32)
        for j, c in enumerate(self.z_copies):
            c.wait()
            total = total + self.z[j].astype(F32)
        self.full[place["x"]] = total.astype(BF)

    def gather_start(self):
        place = self.place
        mine = self.full.at[place["x"]]
        self.gather_copies = [
            self.copy(mine, mine, place["at"](x=lax.rem(place["x"] + j, NX))) for j in range(1, NX)
        ]

    def gather_done(self):
        for c in self.gather_copies:
            c.wait()

    def matrix(self, tile):
        return [self.full[q, :, tile * 128 : (tile + 1) * 128].astype(F32) for q in range(NX)]


    def cross(self, stage, half, axis, i):
        part = pl.ds(half * HALF, HALF)
        y, x = self.place["y"], self.place["x"]
        if stage == 0:
            return self.held.at[i, :, part] if axis == "y" else self.held.at[:, i, part]
        return self.held.at[i, x, part] if axis == "y" else self.held.at[y, i, part]

    def plane_start(self, stage):
        place = self.place
        self.plane = []
        for half, axis in enumerate(("y", "x") if stage == 0 else ("x", "y")):
            for j in range(1, 4):
                there = lax.rem(place[axis] + j, 4)
                self.plane.append(
                    self.copy(self.cross(stage, half, axis, there), self.land[stage].at[half, j - 1],
                              place["at"](**{axis: there}))
                )

    def plane_done(self, stage):
        place = self.place
        for c in self.plane:
            c.wait()
        for half, axis in enumerate(("y", "x") if stage == 0 else ("x", "y")):
            add(self.cross(stage, half, axis, place[axis]), *[self.land[stage].at[half, j] for j in range(3)])


class Gains:
    def __init__(self, refs, place):
        self.sums, self.land, self.send, self.recv = refs
        self.place = place

    def start(self, stage):
        place = self.place
        first = (0, 1, 4, 7)[stage]
        peers = []
        if stage == 0:
            peers = [place["at"](core=1 - place["core"])]
        elif stage < 3:
            axis = "yx"[stage - 1]
            peers = [place["at"](**{axis: lax.rem(place[axis] + j, 4)}) for j in range(1, 4)]
        else:
            z = place["zh"] * NZL + place["zl"]
            for j in range(1, NZ):
                there = lax.rem(z + j, NZ)
                peers.append(place["at"](zh=there // NZL, zl=lax.rem(there, NZL)))
        self.copies = []
        for i, peer in enumerate(peers):
            c = pltpu.make_async_remote_copy(
                src_ref=self.sums.at[stage], dst_ref=self.land.at[first + i], send_sem=self.send.at[first + i],
                recv_sem=self.recv.at[first + i], device_id=peer, device_id_type=MESH,
            )
            c.start()
            self.copies.append(c)

    def done(self, stage):
        first = (0, 1, 4, 7)[stage]
        total = self.sums[stage]
        for i, c in enumerate(self.copies):
            c.wait()
            total = total + self.land[first + i]
        self.sums[stage + 1] = total


def bundle_scratch(tiles):
    c = tiles * 128
    copies = 1 + 6 + 6 + (NZ - 1) + (NX - 1)
    return [
        pltpu.VMEM((NCORE, NY, NX, NZH, SHARE, c), BF),
        pltpu.VMEM((NY, NX, NZH, SHARE, c), BF),
        pltpu.VMEM((NZ - 1, SHARE, c), BF),
        pltpu.VMEM((NX, SHARE, c), BF),
        pltpu.SemaphoreType.DMA((copies,)),
        pltpu.SemaphoreType.DMA((copies,)),
        pltpu.VMEM((2, 3, 4, HALF, SHARE, c), BF),
        pltpu.VMEM((2, 3, HALF, SHARE, c), BF),
    ]


def kernel(
    lat_in, up_in, wm_in, ws_in, wa_in, wo_in, gains_in, edge_in, nbr_in, sends_in,
    lat_out, grad_out, gm_out, gs_out, ga_out, go_out, gg_out,
    xs, up, wm, ws, wa, wo, gains, edge, nbr, sends, adj, own, xh, mh, out_blocks, back, ret0, ret1,
    pm, pmh, ph, normed, inverse, merged, hidden, acc, acc2, gy, gu, gph, gmg, gpm, gpmh, in_sem, out_sem,
    halo_send, halo_recv, gain_sums, gain_land, gain_send, gain_recv, *bundle_refs,
):
    space = lax.axis_index("space")
    slab = lax.axis_index("slab")
    core = lax.rem(space, NCORE)
    zh = lax.rem(space // NCORE, NZH)
    y = space // (NCORE * NZH)
    zl = lax.rem(slab, NZL)
    x = slab // NZL

    def at(**new):
        p = {"core": core, "zh": zh, "y": y, "zl": zl, "x": x, **new}
        return ((p["y"] * NZH + p["zh"]) * NCORE + p["core"], p["x"] * NZL + p["zl"])

    place = {"core": core, "zh": zh, "y": y, "zl": zl, "x": x, "at": at}
    s_up, s_down = lax.rem(space + 1, N_SPACE), lax.rem(space + N_SPACE - 1, N_SPACE)
    l_up, l_down = lax.rem(slab + 1, N_SLAB), lax.rem(slab + N_SLAB - 1, N_SLAB)
    ahead = [(s_up, slab), (s_down, slab), (space, l_up), (space, l_down)]
    behind = [ahead[1], ahead[0], ahead[3], ahead[2]]

    barrier = pltpu.get_barrier_semaphore()
    partners = list(ahead) + [at(core=1 - core)]
    partners += [at(y=lax.rem(y + i, NY), x=lax.rem(x + j, NX)) for i in range(NY) for j in range(NX) if i or j]
    z = zh * NZL + zl
    for j in range(1, NZ):
        there = lax.rem(z + j, NZ)
        partners.append(at(zh=there // NZL, zl=lax.rem(there, NZL)))
    for p in partners:
        pl.semaphore_signal(barrier, inc=1, device_id=p, device_id_type=MESH)

    pairs = [
        (lat_in, xs.at[0]), (sends_in.at[0, 0], sends), (wm_in, wm), (nbr_in, nbr), (edge_in, edge), (ws_in, ws),
        (wa_in, wa), (wo_in, wo), (gains_in, gains), (up_in, up),
    ]
    loads = [pltpu.make_async_copy(a, b, in_sem.at[i]) for i, (a, b) in enumerate(pairs)]
    for c in loads:
        c.start()
    lat_load, sends_load, wm_load, nbr_load, edge_load, ws_load, wa_load, wo_load, gains_load, up_load = loads

    count = len(bundle_scratch(1))
    bundles = [Bundle(bundle_refs[i * count : (i + 1) * count], place) for i in range(2 * LAYERS)]
    ret = (ret0, ret1)
    gain = Gains((gain_sums, gain_land, gain_send, gain_recv), place)

    def halo(src, dst, peers, exchange, before):
        copies = {}
        for d in ORDER:
            before(d)
            copies[d] = pltpu.make_async_remote_copy(
                src_ref=src(d), dst_ref=dst(d), send_sem=halo_send.at[exchange, d],
                recv_sem=halo_recv.at[exchange, d], device_id=peers[d], device_id_type=MESH,
            )
            copies[d].start()
        return copies

    def adjacency(e, blocks, rows=slice(None)):
        return jnp.concatenate([adj[e + j, rows] for j in range(blocks)], axis=1)

    def halo_rows(d):
        return slice(d * HALO_ROWS, (d + 1) * HALO_ROWS)

    def picked(l):
        def pick(d):
            for t in range(2):
                out_blocks[l, d, block_rows(t)] = xs[l, sends[t, d]]

        return pick

    lat_load.wait()
    sends_load.wait()
    pl.semaphore_wait(barrier, len(partners))
    wide = [slice(i * 256, (i + 1) * 256) for i in range(ROWS // 256)]

    def update_grad(l, cotangent):
        row = jnp.zeros((1, W), F32)
        for r in wide:
            g = cotangent(r)
            n = normed[l, r]
            row = row + jnp.sum(g * n, axis=0, keepdims=True)
            g = g * gains[l : l + 1, :]
            u = g - jnp.mean(g, axis=-1, keepdims=True) - n * jnp.mean(g * n, axis=-1, keepdims=True)
            gu[l, r] = (inverse[l, r] * u).astype(BF)
        for r in wide:
            gph[l, r] = (dot(gu[l, r], wo[l], 1, 1) * ph[l, r]).astype(BF)
        for r in wide:
            gmg[r] = dot(gph[l, r], wa[l], 1, 1).astype(BF)
        gain_sums[0, l : l + 1, :] = row

    for l in range(LAYERS):
        copies = halo(
            lambda d: out_blocks.at[l, d], lambda d: xh.at[l, pl.ds(d * HALO_ROWS, HALO_ROWS)], ahead, l, picked(l)
        )
        if l == 0:
            wm_load.wait()
        for b in range(OWN):
            r = block_rows(b)
            v = dot(xs[l, b], wm[l], 1, 0)
            s = sigmoid(v)
            own[r] = (v * s).astype(BF)
            pm[l, r] = slope(v, s)
        if l == 0:
            edge_load.wait()
            nbr_load.wait()

            def build(i):
                b = i // SLOTS
                e = lax.rem(i, SLOTS)
                total = jnp.zeros((BLOCK, BLOCK), F32)
                for k in range(TILES):
                    keep = jnp.where(nbr[b, k] == e, 1.0, 0.0)
                    total = total + edge[b, k].astype(F32) * keep
                adj[e, rows_of(b, BLOCK), :] = total.astype(BF)

            loop(OWN * SLOTS, build)
            for c in (ws_load, wa_load, wo_load, gains_load, up_load):
                c.wait()
        for b in range(OWN):
            r = block_rows(b)
            ph[l, r] = dot(xs[l, b], ws[l], 1, 0)
            acc[r] = dot(adjacency(0, OWN, r), own[...], 1, 0)
        if l > 0:
            for i in range(4 * HALO_ROWS // BLOCK):
                r = block_rows(i)
                v = pmh[l - 1, r]
                pmh[l - 1, r] = slope(v, sigmoid(v))
        for d in ORDER_IN:
            copies[d].wait()
            for t in range(2):
                r = slice(d * HALO_ROWS + t * BLOCK, d * HALO_ROWS + (t + 1) * BLOCK)
                v = dot(xh[l, r], wm[l], 1, 0)
                pmh[l, r] = v
                mh[r] = (v * sigmoid(v)).astype(BF)
            if d != ORDER_IN[-1]:
                for b in range(OWN):
                    r = block_rows(b)
                    acc[r] += dot(adjacency(OWN + 2 * d, 2, r), mh[halo_rows(d)], 1, 0)
        d = ORDER_IN[-1]
        last = mh[halo_rows(d)]
        for b in range(OWN):
            r = block_rows(b)
            merged[l, r] = (acc[r] + dot(adjacency(OWN + 2 * d, 2, r), last, 1, 0)).astype(BF)
        for b in range(OWN):
            r = block_rows(b)
            v = ph[l, r] + dot(merged[l, r], wa[l], 1, 0)
            s = sigmoid(v)
            hidden[l, r] = (v * s).astype(BF)
            ph[l, r] = slope(v, s)
        updates = [dot(hidden[l, block_rows(b)], wo[l], 1, 0) for b in range(OWN)]
        for b, u in enumerate(updates):
            r = block_rows(b)
            centred = u - jnp.mean(u, axis=-1, keepdims=True)
            inv = lax.rsqrt(jnp.mean(centred * centred, axis=-1, keepdims=True) + EPS)
            n = centred * inv
            xs[l + 1, b] = (xs[l, b].astype(F32) + gains[l : l + 1, :] * n).astype(BF)
            normed[l, r] = n
            inverse[l, r] = inv

    update_grad(LAYERS - 1, lambda r: up[r].astype(F32))
    out_copy = pltpu.make_async_copy(xs.at[LAYERS], lat_out, out_sem.at[0])
    out_copy.start()

    def weight_grad(bundle, tile, *pairs):
        for i in range(2):
            r = pl.ds(i * 256, 256)
            v = sum(dot(a(r), g[...], 0, 0) for a, g in pairs)
            v = v.astype(BF).reshape(2, NZH, NCORE, SHARE, W)
            for c in range(NCORE):
                for q in range(NX):
                    bundle.grad[c, pl.ds(2 * i, 2), q, :, :, tile * 128 : (tile + 1) * 128] = v[
                        :, :, c, :, q * 128 : (q + 1) * 128
                    ]

    def put(out, l, bundle, tile):
        for q, v in enumerate(bundle.matrix(tile)):
            out[l, :, q * 128 : (q + 1) * 128] = v

    def put_gains():
        pick = lax.broadcasted_iota(jnp.int32, (W, SHARE), 0) - space * SHARE
        pick = (pick == lax.broadcasted_iota(jnp.int32, (W, SHARE), 1)).astype(F32)
        gg_out[...] = lax.dot_general(
            gain_sums[4], pick, (((1,), (0,)), ((), ())), precision=lax.Precision.HIGHEST, preferred_element_type=F32
        )

    def put_all(l, one, two):
        one.gather_done()
        put(go_out, l, one, 0)
        put(gs_out, l, one, 1)
        two.gather_done()
        put(ga_out, l, two, 0)
        put(gm_out, l, two, 1)

    def z_to_gather(one, two):
        for bundle in (one, two):
            bundle.z_done()
            bundle.gather_start()

    earlier = None
    for l in reversed(range(LAYERS)):

        def back_grad(d, l=l):
            v = dot(adjacency(OWN + 2 * d, 2), gmg[...], 0, 0)
            back[l, d] = v.astype(BF).reshape(2, BLOCK, W)

        copies = halo(
            lambda d: back.at[l, d], lambda d: ret[l].at[d, pl.ds(0, 2)], behind, LAYERS + l, back_grad
        )

        one, two = bundles[2 * l], bundles[2 * l + 1]
        if earlier:
            gain.start(0)
            for bundle in earlier:
                bundle.plane_done(0)
                bundle.plane_start(1)

        def latent_columns(r, l=l):
            return xs[l, :, :, r].reshape(ROWS, 256)

        weight_grad(one, 0, (lambda r: hidden[l, :, r], gu.at[l]))
        weight_grad(one, 1, (latent_columns, gph.at[l]))
        one.core_start()
        for b in range(OWN):
            r = block_rows(b)
            v = dot(adj[b], gmg[...], 0, 0)
            acc2[r] = v
            gpm[r] = (v * pm[l, r]).astype(BF)
        for i in range(4 * HALO_ROWS // BLOCK):
            r = block_rows(i)
            v = pmh[l, r]
            if l == LAYERS - 1:
                v = slope(v, sigmoid(v))
            gpmh[r] = (back[l, i // 2, i % 2].astype(F32) * v).astype(BF)
        weight_grad(two, 0, (lambda r: merged[l, :, r], gph.at[l]))
        weight_grad(two, 1, (latent_columns, gpm), (lambda r: xh[l, :, r], gpmh))
        two.core_start()
        if earlier:
            for bundle in earlier:
                bundle.plane_done(1)
                bundle.z_start()
            gain.done(0)
            gain.start(1)
        for d in range(4):
            ret[l][d, 2] = jnp.zeros((BLOCK, W), BF)
        one.core_done()
        one.plane_start(0)
        for b in range(OWN):
            r = block_rows(b)
            before = up[r].astype(F32) if l == LAYERS - 1 else gy[r]
            gy[r] = before + dot(gph[l, r], ws[l], 1, 1)
        two.core_done()
        two.plane_start(0)
        if earlier:
            gain.done(1)
            gain.start(2)
            z_to_gather(*earlier)
            for bundle in (one, two):
                bundle.plane_done(0)
                bundle.plane_start(1)
            gain.done(2)
            gain.start(3)
            put_all(l + 1, *earlier)
            for bundle in (one, two):
                bundle.plane_done(1)
                bundle.z_start()
        for d in ORDER:
            copies[d].wait()

        def message_grad(b, l=l):
            r = block_rows(b)
            total = acc2[r]
            for d in range(4):
                which = jnp.where(sends[0, d] == b, 0, jnp.where(sends[1, d] == b, 1, 2))
                total = total + ret[l][d, which].astype(F32)
            gpm[r] = (total * pm[l, r]).astype(BF)

        for b in range(OWN):
            message_grad(b)
        for r in wide:
            gy[r] += dot(gpm[r], wm[l], 1, 1)
        if l > 0:
            update_grad(l - 1, lambda r: gy[r])
        earlier = (one, two)

    grad_copy = pltpu.make_async_copy(gy, grad_out, out_sem.at[1])
    grad_copy.start()
    z_to_gather(*earlier)
    gain.done(3)
    put_gains()
    put_all(0, *earlier)
    out_copy.wait()
    grad_copy.wait()


PIECES = (2, 4, 1, 1, 1, 1, 1)


def hand_over(*refs):
    count = len(PIECES)
    into, out, held = refs[:count], refs[count : 2 * count], refs[2 * count : 3 * count]
    in_sem, out_sem = refs[3 * count :]
    steps = []
    for i, pieces in enumerate(PIECES):
        size = into[i].shape[0] // pieces
        for j in range(pieces):
            piece = pl.ds(j * size, size)
            n = len(steps)
            steps.append((
                pltpu.make_async_copy(into[i].at[piece], held[i].at[piece], in_sem.at[n]),
                pltpu.make_async_copy(held[i].at[piece], out[i].at[piece], out_sem.at[n]),
            ))
    for first, _ in steps:
        first.start()
    for first, second in steps:
        first.wait()
        second.start()
    for _, second in steps:
        second.wait()


def local(
    latents, upstream, msg_weight, self_weight, agg_weight, out_weight, gains, edge_weight, nbr_slot, send_list
):
    hbm = pl.BlockSpec(memory_space=pl.ANY)
    vmem = pl.BlockSpec(memory_space=pltpu.VMEM)
    share = jax.ShapeDtypeStruct((LAYERS, SHARE, W), F32)
    scratch = [
        pltpu.VMEM((LAYERS + 1, OWN, BLOCK, W), BF),
        pltpu.VMEM((ROWS, W), BF),
        pltpu.VMEM((LAYERS, W, W), BF),
        pltpu.VMEM((LAYERS, W, W), BF),
        pltpu.VMEM((LAYERS, W, W), BF),
        pltpu.VMEM((LAYERS, W, W), BF),
        pltpu.VMEM((LAYERS, W), F32),
        pltpu.VMEM((OWN, TILES, BLOCK, BLOCK), BF),
        pltpu.SMEM((OWN, TILES), jnp.int32),
        pltpu.SMEM((2, 4), jnp.int32),
        pltpu.VMEM((SLOTS, ROWS, BLOCK), BF),
        pltpu.VMEM((ROWS, W), BF),
        pltpu.VMEM((LAYERS, 4 * HALO_ROWS, W), BF),
        pltpu.VMEM((4 * HALO_ROWS, W), BF),
        pltpu.VMEM((LAYERS, 4, HALO_ROWS, W), BF),
        pltpu.VMEM((LAYERS, 4, 2, BLOCK, W), BF),
        pltpu.VMEM((4, 3, BLOCK, W), BF),
        pltpu.VMEM((4, 3, BLOCK, W), BF),
        pltpu.VMEM((LAYERS, ROWS, W), F32),
        pltpu.VMEM((LAYERS, 4 * HALO_ROWS, W), F32),
        pltpu.VMEM((LAYERS, ROWS, W), F32),
        pltpu.VMEM((LAYERS, ROWS, W), F32),
        pltpu.VMEM((LAYERS, ROWS, 1), F32),
        pltpu.VMEM((LAYERS, ROWS, W), BF),
        pltpu.VMEM((LAYERS, ROWS, W), BF),
        pltpu.VMEM((ROWS, W), F32),
        pltpu.VMEM((ROWS, W), F32),
        pltpu.VMEM((ROWS, W), F32),
        pltpu.VMEM((LAYERS, ROWS, W), BF),
        pltpu.VMEM((LAYERS, ROWS, W), BF),
        pltpu.VMEM((ROWS, W), BF),
        pltpu.VMEM((ROWS, W), BF),
        pltpu.VMEM((4 * HALO_ROWS, W), BF),
        pltpu.SemaphoreType.DMA((10,)),
        pltpu.SemaphoreType.DMA((2,)),
        pltpu.SemaphoreType.DMA((2 * LAYERS, 4)),
        pltpu.SemaphoreType.DMA((2 * LAYERS, 4)),
        pltpu.VMEM((5, LAYERS, W), F32),
        pltpu.VMEM((14, LAYERS, W), F32),
        pltpu.SemaphoreType.DMA((14,)),
        pltpu.SemaphoreType.DMA((14,)),
    ]
    for tiles in BUNDLE_TILES * LAYERS:
        scratch += bundle_scratch(tiles)
    shapes = (
        jax.ShapeDtypeStruct((OWN, BLOCK, W), BF),
        jax.ShapeDtypeStruct((ROWS, W), F32),
        share, share, share, share,
        jax.ShapeDtypeStruct((LAYERS, SHARE), F32),
    )
    out = pl.pallas_call(
        kernel,
        out_shape=shapes,
        in_specs=[hbm] * 10,
        out_specs=(hbm, hbm, vmem, vmem, vmem, vmem, vmem),
        scratch_shapes=scratch,
        compiler_params=pltpu.CompilerParams(
            collective_id=0, has_side_effects=True, vmem_limit_bytes=60 * 1024 * 1024
        ),
        cost_estimate=pl.CostEstimate(flops=10 * 10**9, bytes_accessed=10 * 2**20, transcendentals=2 * 10**6),
    )(latents.reshape(OWN, BLOCK, W), upstream, msg_weight, self_weight, agg_weight, out_weight, gains, edge_weight, nbr_slot, jnp.swapaxes(send_list, 2, 3))
    first, *rest = pl.pallas_call(
        hand_over,
        out_shape=shapes,
        in_specs=[hbm] * 7,
        out_specs=[hbm] * 7,
        scratch_shapes=[pltpu.VMEM(v.shape, v.dtype) for v in shapes]
        + [pltpu.SemaphoreType.DMA((sum(PIECES),)), pltpu.SemaphoreType.DMA((sum(PIECES),))],
    )(*out)
    return (first.reshape(ROWS, W), *rest)


def solution(mesh):
    rows = P(("space", "slab"), None)
    return jax.shard_map(
        local,
        mesh=mesh,
        in_specs=(
            rows, rows, P(), P(), P(), P(), P(),
            P(("space", "slab"), None, None, None), rows, P("space", "slab", None, None),
        ),
        out_specs=(
            rows, rows, P(None, "space", None), P(None, "space", None), P(None, "space", None),
            P(None, "space", None), P(None, "space"),
        ),
        check_vma=False,
    )
```

```python
import jax
import jax.numpy as jnp
from jax import lax
from jax.experimental import pallas as pl
from jax.experimental.pallas import tpu as pltpu
from jax.sharding import PartitionSpec as P

EPS = 1e-05
BF = jnp.bfloat16
F32 = jnp.float32
MESH = pl.DeviceIdType.MESH

W = 512
BLOCK = 128
OWN = 4
TILES = 6
SLOTS = 12
ROWS = OWN * BLOCK
COLS = SLOTS * BLOCK
LAYERS = 2
NY, NZH, NCORE = 4, 4, 2
NX, NZL = 4, 2
NZ = NZH * NZL
N_SPACE = NY * NZH * NCORE
N_SLAB = NX * NZL
SHARE = W // N_SPACE

BUNDLE_TILES = (2, 2)
ORDER = (0, 1, 2, 3)
ORDER_IN = (0, 1, 2, 3)
Y_FIRST = (3, 3)
HALO_ROWS = 2 * BLOCK


def sigmoid(v):
    return 0.5 * jnp.tanh(0.5 * v) + 0.5


def slope(v, s):
    return s * (1.0 + v * (1.0 - s))


def dot(a, b, ca, cb):
    return lax.dot_general(a, b, (((ca,), (cb,)), ((), ())), preferred_element_type=F32)


def loop(count, body):
    def step(i, carry):
        body(i)
        return carry

    lax.fori_loop(0, count, step, 0)


def rows_of(i, size):
    return pl.ds(pl.multiple_of(i * size, size), size)


def block_rows(b):
    return slice(b * BLOCK, (b + 1) * BLOCK)


def add(dst, *others):
    total = dst[...].astype(F32)
    for other in others:
        total = total + other[...].astype(F32)
    dst[...] = total.astype(BF)


class Bundle:
    def __init__(self, refs, place, y_first):
        self.y_first = y_first
        self.grad, self.held, self.z, self.full, self.send, self.recv, *self.land = refs
        self.place = place
        self.next = 0

    def copy(self, src, dst, device):
        i = self.next
        self.next += 1
        c = pltpu.make_async_remote_copy(
            src_ref=src, dst_ref=dst, send_sem=self.send.at[i], recv_sem=self.recv.at[i],
            device_id=device, device_id_type=MESH,
        )
        c.start()
        return c

    def core_start(self):
        core = self.place["core"]
        self.core_copy = self.copy(self.grad.at[1 - core], self.held, self.place["at"](core=1 - core))

    def core_done(self):
        core = self.place["core"]
        self.core_copy.wait()

        def body(i):
            self.held[i] = (self.held[i].astype(F32) + self.grad[core, i].astype(F32)).astype(BF)

        loop(NY, body)

    def z_start(self):
        place = self.place
        z = place["zh"] * NZL + place["zl"]
        self.z_copies = []
        for j in range(1, NZ):
            there = lax.rem(z + j, NZ)
            zh, zl = there // NZL, lax.rem(there, NZL)
            self.z_copies.append(
                self.copy(self.held.at[place["y"], place["x"], zh, :, rows_of(zl, 128)], self.z.at[j - 1],
                          place["at"](zh=zh, zl=zl))
            )

    def z_done(self):
        place = self.place
        total = self.held[place["y"], place["x"], place["zh"], :, rows_of(place["zl"], 128)].astype(F32)
        for j, c in enumerate(self.z_copies):
            c.wait()
            total = total + self.z[j].astype(F32)
        self.full[place["x"], place["zl"]] = total.astype(BF)

    def gather_start(self):
        place = self.place
        mine = self.full.at[place["x"], place["zl"]]
        slab = place["x"] * NZL + place["zl"]
        self.gather_copies = []
        for j in range(1, N_SLAB):
            there = lax.rem(slab + j, N_SLAB)
            self.gather_copies.append(self.copy(mine, mine, place["at"](x=there // NZL, zl=lax.rem(there, NZL))))

    def gather_done(self):
        for c in self.gather_copies:
            c.wait()

    def matrix(self, tile):
        return [self.full[q, tile].astype(F32) for q in range(NX)]


    def ways(self, stage):
        cut = self.y_first
        ways = [("yx"[stage], pl.ds(0, cut))]
        if cut < NZH:
            ways.append(("xy"[stage], pl.ds(cut, NZH - cut)))
        return ways

    def cross(self, stage, part, axis, i):
        y, x = self.place["y"], self.place["x"]
        if stage == 0:
            return self.held.at[i, :, part] if axis == "y" else self.held.at[:, i, part]
        return self.held.at[i, x, part] if axis == "y" else self.held.at[y, i, part]

    def landing(self, stage, part, j):
        if stage == 0:
            return self.land[0].at[j, :, part]
        return self.land[1].at[j, part]

    def plane_start(self, stage):
        place = self.place
        self.plane = []
        for axis, part in self.ways(stage):
            for j in range(1, 4):
                there = lax.rem(place[axis] + j, 4)
                self.plane.append(
                    self.copy(self.cross(stage, part, axis, there), self.landing(stage, part, j - 1),
                              place["at"](**{axis: there}))
                )

    def plane_done(self, stage):
        for c in self.plane:
            c.wait()
        for axis, part in self.ways(stage):
            add(self.cross(stage, part, axis, self.place[axis]), *[self.landing(stage, part, j) for j in range(3)])


class Gains:
    def __init__(self, refs, place):
        self.sums, self.land, self.send, self.recv = refs
        self.place = place

    def start(self, stage):
        place = self.place
        first = (0, 1, 4, 7)[stage]
        peers = []
        if stage == 0:
            peers = [place["at"](core=1 - place["core"])]
        elif stage < 3:
            axis = "yx"[stage - 1]
            peers = [place["at"](**{axis: lax.rem(place[axis] + j, 4)}) for j in range(1, 4)]
        else:
            z = place["zh"] * NZL + place["zl"]
            for j in range(1, NZ):
                there = lax.rem(z + j, NZ)
                peers.append(place["at"](zh=there // NZL, zl=lax.rem(there, NZL)))
        self.copies = []
        for i, peer in enumerate(peers):
            c = pltpu.make_async_remote_copy(
                src_ref=self.sums.at[stage], dst_ref=self.land.at[first + i], send_sem=self.send.at[first + i],
                recv_sem=self.recv.at[first + i], device_id=peer, device_id_type=MESH,
            )
            c.start()
            self.copies.append(c)

    def done(self, stage):
        first = (0, 1, 4, 7)[stage]
        total = self.sums[stage]
        for i, c in enumerate(self.copies):
            c.wait()
            total = total + self.land[first + i]
        self.sums[stage + 1] = total


def bundle_scratch(tiles):
    c = tiles * 128
    copies = 1 + 6 + 6 + (NZ - 1) + (N_SLAB - 1)
    return [
        pltpu.VMEM((NCORE, NY, NX, NZH, SHARE, c), BF),
        pltpu.VMEM((NY, NX, NZH, SHARE, c), BF),
        pltpu.VMEM((NZ - 1, SHARE, 128), BF),
        pltpu.VMEM((NX, NZL, SHARE, 128), BF),
        pltpu.SemaphoreType.DMA((copies,)),
        pltpu.SemaphoreType.DMA((copies,)),
        pltpu.VMEM((3, 4, NZH, SHARE, c), BF),
        pltpu.VMEM((3, NZH, SHARE, c), BF),
    ]


def kernel(
    lat_in, up_in, wm_in, ws_in, wa_in, wo_in, gains_in, edge_in, nbr_in, sends_in,
    lat_out, grad_out, gm_out, gs_out, ga_out, go_out, gg_out,
    xs, up, wm, ws, wa, wo, gains, edge, nbr, sends, adj, own, xh, mh, out_blocks, back, ret0, ret1,
    pm, pmh, ph, normed, inverse, merged, hidden, acc, acc2, gy, gu, gph, gmg, gpm, gpmh, in_sem, out_sem,
    halo_send, halo_recv, gain_sums, gain_land, gain_send, gain_recv, *bundle_refs,
):
    space = lax.axis_index("space")
    slab = lax.axis_index("slab")
    core = lax.rem(space, NCORE)
    zh = lax.rem(space // NCORE, NZH)
    y = space // (NCORE * NZH)
    zl = lax.rem(slab, NZL)
    x = slab // NZL

    def at(**new):
        p = {"core": core, "zh": zh, "y": y, "zl": zl, "x": x, **new}
        return ((p["y"] * NZH + p["zh"]) * NCORE + p["core"], p["x"] * NZL + p["zl"])

    place = {"core": core, "zh": zh, "y": y, "zl": zl, "x": x, "at": at}
    s_up, s_down = lax.rem(space + 1, N_SPACE), lax.rem(space + N_SPACE - 1, N_SPACE)
    l_up, l_down = lax.rem(slab + 1, N_SLAB), lax.rem(slab + N_SLAB - 1, N_SLAB)
    ahead = [(s_up, slab), (s_down, slab), (space, l_up), (space, l_down)]
    behind = [ahead[1], ahead[0], ahead[3], ahead[2]]

    barrier = pltpu.get_barrier_semaphore()
    partners = list(ahead) + [at(core=1 - core)]
    partners += [at(y=lax.rem(y + j, NY)) for j in range(1, NY)]
    for j in range(1, N_SLAB):
        there = lax.rem(slab + j, N_SLAB)
        partners.append(at(x=there // NZL, zl=lax.rem(there, NZL)))
    z = zh * NZL + zl
    for j in range(1, NZ):
        there = lax.rem(z + j, NZ)
        partners.append(at(zh=there // NZL, zl=lax.rem(there, NZL)))
    for p in partners:
        pl.semaphore_signal(barrier, inc=1, device_id=p, device_id_type=MESH)

    pairs = [
        (lat_in, xs.at[0]), (sends_in.at[0, 0], sends), (wm_in, wm), (nbr_in, nbr), (edge_in, edge), (ws_in, ws),
        (wa_in, wa), (wo_in, wo), (gains_in, gains), (up_in, up),
    ]
    loads = [pltpu.make_async_copy(a, b, in_sem.at[i]) for i, (a, b) in enumerate(pairs)]
    for c in loads:
        c.start()
    lat_load, sends_load, wm_load, nbr_load, edge_load, ws_load, wa_load, wo_load, gains_load, up_load = loads

    count = len(bundle_scratch(1))
    bundles = [Bundle(bundle_refs[i * count : (i + 1) * count], place, Y_FIRST[i // 2])
               for i in range(2 * LAYERS)]
    ret = (ret0, ret1)
    gain = Gains((gain_sums, gain_land, gain_send, gain_recv), place)

    def halo(src, dst, peers, exchange, before):
        copies = {}
        for d in ORDER:
            before(d)
            copies[d] = pltpu.make_async_remote_copy(
                src_ref=src(d), dst_ref=dst(d), send_sem=halo_send.at[exchange, d],
                recv_sem=halo_recv.at[exchange, d], device_id=peers[d], device_id_type=MESH,
            )
            copies[d].start()
        return copies

    def adjacency(e, blocks, rows=slice(None)):
        return jnp.concatenate([adj[e + j, rows] for j in range(blocks)], axis=1)

    def halo_rows(d):
        return slice(d * HALO_ROWS, (d + 1) * HALO_ROWS)

    def picked(l):
        def pick(d):
            for t in range(2):
                out_blocks[l, d, block_rows(t)] = xs[l, sends[t, d]]

        return pick

    lat_load.wait()
    sends_load.wait()
    pl.semaphore_wait(barrier, len(partners))
    wide = [slice(i * 256, (i + 1) * 256) for i in range(ROWS // 256)]

    def update_grad(l, cotangent):
        row = jnp.zeros((1, W), F32)
        for r in wide:
            g = cotangent(r)
            n = normed[l, r]
            row = row + jnp.sum(g * n, axis=0, keepdims=True)
            g = g * gains[l : l + 1, :]
            u = g - jnp.mean(g, axis=-1, keepdims=True) - n * jnp.mean(g * n, axis=-1, keepdims=True)
            gu[l, r] = (inverse[l, r] * u).astype(BF)
        for r in wide:
            gph[l, r] = (dot(gu[l, r], wo[l], 1, 1) * ph[l, r]).astype(BF)
        for r in wide:
            gmg[r] = dot(gph[l, r], wa[l], 1, 1).astype(BF)
        gain_sums[0, l : l + 1, :] = row

    for l in range(LAYERS):
        copies = halo(
            lambda d: out_blocks.at[l, d], lambda d: xh.at[l, pl.ds(d * HALO_ROWS, HALO_ROWS)], ahead, l, picked(l)
        )
        if l == 0:
            wm_load.wait()
        for b in range(OWN):
            r = block_rows(b)
            v = dot(xs[l, b], wm[l], 1, 0)
            s = sigmoid(v)
            own[r] = (v * s).astype(BF)
            pm[l, r] = slope(v, s)
        if l == 0:
            edge_load.wait()
            nbr_load.wait()

            def build(i):
                b = i // SLOTS
                e = lax.rem(i, SLOTS)
                total = jnp.zeros((BLOCK, BLOCK), F32)
                for k in range(TILES):
                    keep = jnp.where(nbr[b, k] == e, 1.0, 0.0)
                    total = total + edge[b, k].astype(F32) * keep
                adj[e, rows_of(b, BLOCK), :] = total.astype(BF)

            loop(OWN * SLOTS, build)
            for c in (ws_load, wa_load, wo_load, gains_load, up_load):
                c.wait()
        for b in range(OWN):
            r = block_rows(b)
            ph[l, r] = dot(xs[l, b], ws[l], 1, 0)
            acc[r] = dot(adjacency(0, OWN, r), own[...], 1, 0)
        if l > 0:
            for i in range(4 * HALO_ROWS // BLOCK):
                r = block_rows(i)
                v = pmh[l - 1, r]
                pmh[l - 1, r] = slope(v, sigmoid(v))
        for d in ORDER_IN:
            copies[d].wait()
            for t in range(2):
                r = slice(d * HALO_ROWS + t * BLOCK, d * HALO_ROWS + (t + 1) * BLOCK)
                v = dot(xh[l, r], wm[l], 1, 0)
                pmh[l, r] = v
                mh[r] = (v * sigmoid(v)).astype(BF)
            if d != ORDER_IN[-1]:
                for b in range(OWN):
                    r = block_rows(b)
                    acc[r] += dot(adjacency(OWN + 2 * d, 2, r), mh[halo_rows(d)], 1, 0)
        d = ORDER_IN[-1]
        last = mh[halo_rows(d)]
        for b in range(OWN):
            r = block_rows(b)
            merged[l, r] = (acc[r] + dot(adjacency(OWN + 2 * d, 2, r), last, 1, 0)).astype(BF)
        for b in range(OWN):
            r = block_rows(b)
            v = ph[l, r] + dot(merged[l, r], wa[l], 1, 0)
            s = sigmoid(v)
            hidden[l, r] = (v * s).astype(BF)
            ph[l, r] = slope(v, s)
        updates = [dot(hidden[l, block_rows(b)], wo[l], 1, 0) for b in range(OWN)]
        for b, u in enumerate(updates):
            r = block_rows(b)
            centred = u - jnp.mean(u, axis=-1, keepdims=True)
            inv = lax.rsqrt(jnp.mean(centred * centred, axis=-1, keepdims=True) + EPS)
            n = centred * inv
            xs[l + 1, b] = (xs[l, b].astype(F32) + gains[l : l + 1, :] * n).astype(BF)
            normed[l, r] = n
            inverse[l, r] = inv

    update_grad(LAYERS - 1, lambda r: up[r].astype(F32))
    out_copy = pltpu.make_async_copy(xs.at[LAYERS], lat_out, out_sem.at[0])
    out_copy.start()

    def weight_grad(bundle, tile, *pairs):
        for i in range(2):
            r = pl.ds(i * 256, 256)
            v = sum(dot(a(r), g[...], 0, 0) for a, g in pairs)
            v = v.astype(BF).reshape(2, NZH, NCORE, SHARE, W)
            for c in range(NCORE):
                for q in range(NX):
                    bundle.grad[c, pl.ds(2 * i, 2), q, :, :, tile * 128 : (tile + 1) * 128] = v[
                        :, :, c, :, q * 128 : (q + 1) * 128
                    ]

    def put(out, l, bundle, tile):
        for q, v in enumerate(bundle.matrix(tile)):
            out[l, :, q * 128 : (q + 1) * 128] = v

    def put_gains():
        pick = lax.broadcasted_iota(jnp.int32, (W, SHARE), 0) - space * SHARE
        pick = (pick == lax.broadcasted_iota(jnp.int32, (W, SHARE), 1)).astype(F32)
        gg_out[...] = lax.dot_general(
            gain_sums[4], pick, (((1,), (0,)), ((), ())), precision=lax.Precision.HIGHEST, preferred_element_type=F32
        )

    def put_all(l, one, two):
        one.gather_done()
        put(go_out, l, one, 0)
        put(gs_out, l, one, 1)
        two.gather_done()
        put(ga_out, l, two, 0)
        put(gm_out, l, two, 1)

    def z_to_gather(one, two):
        for bundle in (one, two):
            bundle.z_done()
            bundle.gather_start()

    earlier = None
    for l in reversed(range(LAYERS)):

        def back_grad(d, l=l):
            v = dot(adjacency(OWN + 2 * d, 2), gmg[...], 0, 0)
            back[l, d] = v.astype(BF).reshape(2, BLOCK, W)

        one, two = bundles[2 * l], bundles[2 * l + 1]

        def latent_columns(r, l=l):
            return xs[l, :, :, r].reshape(ROWS, 256)

        def first_grads(l=l):
            weight_grad(one, 0, (lambda r: hidden[l, :, r], gu.at[l]))
            weight_grad(one, 1, (latent_columns, gph.at[l]))
            one.core_start()

        if l == 0:
            first_grads()
            gain.start(0)
        copies = halo(
            lambda d: back.at[l, d], lambda d: ret[l].at[d, pl.ds(0, 2)], behind, LAYERS + l, back_grad
        )

        if l > 0:
            first_grads()
        for b in range(OWN):
            r = block_rows(b)
            v = dot(adj[b], gmg[...], 0, 0)
            acc2[r] = v
            gpm[r] = (v * pm[l, r]).astype(BF)
        for i in range(4 * HALO_ROWS // BLOCK):
            r = block_rows(i)
            v = pmh[l, r]
            if l == LAYERS - 1:
                v = slope(v, sigmoid(v))
            gpmh[r] = (back[l, i // 2, i % 2].astype(F32) * v).astype(BF)
        weight_grad(two, 0, (lambda r: merged[l, :, r], gph.at[l]))
        weight_grad(two, 1, (latent_columns, gpm), (lambda r: xh[l, :, r], gpmh))
        two.core_start()
        one.core_done()
        one.plane_start(0)
        if earlier:
            for bundle in earlier:
                bundle.plane_done(0)
                bundle.plane_start(1)
            gain.done(0)
            gain.start(1)
        for b in range(OWN):
            r = block_rows(b)
            before = up[r].astype(F32) if l == LAYERS - 1 else gy[r]
            gy[r] = before + dot(gph[l, r], ws[l], 1, 1)
        for d in range(4):
            ret[l][d, 2] = jnp.zeros((BLOCK, W), BF)
        two.core_done()
        two.plane_start(0)
        if earlier:
            gain.done(1)
            gain.start(2)
            one.plane_done(0)
            one.plane_start(1)
            for bundle in earlier:
                bundle.plane_done(1)
            two.plane_done(0)
            two.plane_start(1)
            gain.done(2)
            gain.start(3)
            one.plane_done(1)
            one.z_start()
            two.plane_done(1)
            two.z_start()
            for bundle in earlier:
                bundle.z_start()
        for d in ORDER:
            copies[d].wait()

        def message_grad(b, l=l):
            r = block_rows(b)
            total = acc2[r]
            for d in range(4):
                which = jnp.where(sends[0, d] == b, 0, jnp.where(sends[1, d] == b, 1, 2))
                total = total + ret[l][d, which].astype(F32)
            gpm[r] = (total * pm[l, r]).astype(BF)

        for b in range(OWN):
            message_grad(b)
        for r in wide:
            gy[r] += dot(gpm[r], wm[l], 1, 1)
        if l > 0:
            update_grad(l - 1, lambda r: gy[r])
        earlier = (one, two)

    grad_copy = pltpu.make_async_copy(gy, grad_out, out_sem.at[1])
    grad_copy.start()
    gain.done(3)
    z_to_gather(*earlier)
    z_to_gather(*bundles[2 * LAYERS - 2 :])
    put_gains()
    put_all(0, *earlier)
    put_all(LAYERS - 1, *bundles[2 * LAYERS - 2 :])
    out_copy.wait()
    grad_copy.wait()


PIECES = (2, 4, 1, 1, 1, 1, 1)


def hand_over(*refs):
    count = len(PIECES)
    into, out, held = refs[:count], refs[count : 2 * count], refs[2 * count : 3 * count]
    in_sem, out_sem = refs[3 * count :]
    steps = []
    for i, pieces in enumerate(PIECES):
        size = into[i].shape[0] // pieces
        for j in range(pieces):
            piece = pl.ds(j * size, size)
            n = len(steps)
            steps.append((
                pltpu.make_async_copy(into[i].at[piece], held[i].at[piece], in_sem.at[n]),
                pltpu.make_async_copy(held[i].at[piece], out[i].at[piece], out_sem.at[n]),
            ))
    for first, _ in steps:
        first.start()
    for first, second in steps:
        first.wait()
        second.start()
    for _, second in steps:
        second.wait()


def local(
    latents, upstream, msg_weight, self_weight, agg_weight, out_weight, gains, edge_weight, nbr_slot, send_list
):
    hbm = pl.BlockSpec(memory_space=pl.ANY)
    vmem = pl.BlockSpec(memory_space=pltpu.VMEM)
    share = jax.ShapeDtypeStruct((LAYERS, SHARE, W), F32)
    scratch = [
        pltpu.VMEM((LAYERS + 1, OWN, BLOCK, W), BF),
        pltpu.VMEM((ROWS, W), BF),
        pltpu.VMEM((LAYERS, W, W), BF),
        pltpu.VMEM((LAYERS, W, W), BF),
        pltpu.VMEM((LAYERS, W, W), BF),
        pltpu.VMEM((LAYERS, W, W), BF),
        pltpu.VMEM((LAYERS, W), F32),
        pltpu.VMEM((OWN, TILES, BLOCK, BLOCK), BF),
        pltpu.SMEM((OWN, TILES), jnp.int32),
        pltpu.SMEM((2, 4), jnp.int32),
        pltpu.VMEM((SLOTS, ROWS, BLOCK), BF),
        pltpu.VMEM((ROWS, W), BF),
        pltpu.VMEM((LAYERS, 4 * HALO_ROWS, W), BF),
        pltpu.VMEM((4 * HALO_ROWS, W), BF),
        pltpu.VMEM((LAYERS, 4, HALO_ROWS, W), BF),
        pltpu.VMEM((LAYERS, 4, 2, BLOCK, W), BF),
        pltpu.VMEM((4, 3, BLOCK, W), BF),
        pltpu.VMEM((4, 3, BLOCK, W), BF),
        pltpu.VMEM((LAYERS, ROWS, W), F32),
        pltpu.VMEM((LAYERS, 4 * HALO_ROWS, W), F32),
        pltpu.VMEM((LAYERS, ROWS, W), F32),
        pltpu.VMEM((LAYERS, ROWS, W), F32),
        pltpu.VMEM((LAYERS, ROWS, 1), F32),
        pltpu.VMEM((LAYERS, ROWS, W), BF),
        pltpu.VMEM((LAYERS, ROWS, W), BF),
        pltpu.VMEM((ROWS, W), F32),
        pltpu.VMEM((ROWS, W), F32),
        pltpu.VMEM((ROWS, W), F32),
        pltpu.VMEM((LAYERS, ROWS, W), BF),
        pltpu.VMEM((LAYERS, ROWS, W), BF),
        pltpu.VMEM((ROWS, W), BF),
        pltpu.VMEM((ROWS, W), BF),
        pltpu.VMEM((4 * HALO_ROWS, W), BF),
        pltpu.SemaphoreType.DMA((10,)),
        pltpu.SemaphoreType.DMA((2,)),
        pltpu.SemaphoreType.DMA((2 * LAYERS, 4)),
        pltpu.SemaphoreType.DMA((2 * LAYERS, 4)),
        pltpu.VMEM((5, LAYERS, W), F32),
        pltpu.VMEM((14, LAYERS, W), F32),
        pltpu.SemaphoreType.DMA((14,)),
        pltpu.SemaphoreType.DMA((14,)),
    ]
    for tiles in BUNDLE_TILES * LAYERS:
        scratch += bundle_scratch(tiles)
    shapes = (
        jax.ShapeDtypeStruct((OWN, BLOCK, W), BF),
        jax.ShapeDtypeStruct((ROWS, W), F32),
        share, share, share, share,
        jax.ShapeDtypeStruct((LAYERS, SHARE), F32),
    )
    out = pl.pallas_call(
        kernel,
        out_shape=shapes,
        in_specs=[hbm] * 10,
        out_specs=(hbm, hbm, vmem, vmem, vmem, vmem, vmem),
        scratch_shapes=scratch,
        compiler_params=pltpu.CompilerParams(
            collective_id=0, has_side_effects=True, vmem_limit_bytes=60 * 1024 * 1024
        ),
        cost_estimate=pl.CostEstimate(flops=10 * 10**9, bytes_accessed=10 * 2**20, transcendentals=2 * 10**6),
    )(latents.reshape(OWN, BLOCK, W), upstream, msg_weight, self_weight, agg_weight, out_weight, gains, edge_weight, nbr_slot, jnp.swapaxes(send_list, 2, 3))
    first, *rest = pl.pallas_call(
        hand_over,
        out_shape=shapes,
        in_specs=[hbm] * 7,
        out_specs=[hbm] * 7,
        scratch_shapes=[pltpu.VMEM(v.shape, v.dtype) for v in shapes]
        + [pltpu.SemaphoreType.DMA((sum(PIECES),)), pltpu.SemaphoreType.DMA((sum(PIECES),))],
    )(*out)
    return (first.reshape(ROWS, W), *rest)


def solution(mesh):
    rows = P(("space", "slab"), None)
    return jax.shard_map(
        local,
        mesh=mesh,
        in_specs=(
            rows, rows, P(), P(), P(), P(), P(),
            P(("space", "slab"), None, None, None), rows, P("space", "slab", None, None),
        ),
        out_specs=(
            rows, rows, P(None, "space", None), P(None, "space", None), P(None, "space", None),
            P(None, "space", None), P(None, "space"),
        ),
        check_vma=False,
    )
```

```python
import jax
import jax.numpy as jnp
from jax import lax
from jax.experimental import pallas as pl
from jax.experimental.pallas import tpu as pltpu
from jax.sharding import PartitionSpec as P

EPS = 1e-05
BF = jnp.bfloat16
F32 = jnp.float32
MESH = pl.DeviceIdType.MESH

W = 512
BLOCK = 128
OWN = 4
TILES = 6
SLOTS = 12
ROWS = OWN * BLOCK
COLS = SLOTS * BLOCK
LAYERS = 2
NY, NZH, NCORE = 4, 4, 2
NX, NZL = 4, 2
NZ = NZH * NZL
N_SPACE = NY * NZH * NCORE
N_SLAB = NX * NZL
SHARE = W // N_SPACE

BUNDLE_TILES = (2, 2)
ORDER = (0, 1, 2, 3)
ORDER_IN = (0, 1, 2, 3)
Y_FIRST = (3, 3)
HALO_ROWS = 2 * BLOCK


def sigmoid(v):
    return 0.5 * jnp.tanh(0.5 * v) + 0.5


def slope(v, s):
    return s * (1.0 + v * (1.0 - s))


def dot(a, b, ca, cb):
    return lax.dot_general(a, b, (((ca,), (cb,)), ((), ())), preferred_element_type=F32)


def loop(count, body):
    def step(i, carry):
        body(i)
        return carry

    lax.fori_loop(0, count, step, 0)


def rows_of(i, size):
    return pl.ds(pl.multiple_of(i * size, size), size)


def block_rows(b):
    return slice(b * BLOCK, (b + 1) * BLOCK)


def add(dst, *others):
    total = dst[...].astype(F32)
    for other in others:
        total = total + other[...].astype(F32)
    dst[...] = total.astype(BF)


class Bundle:
    def __init__(self, refs, place, y_first):
        self.y_first = y_first
        self.grad, self.held, self.z, self.full, self.send, self.recv, *self.land = refs
        self.place = place
        self.next = 0

    def copy(self, src, dst, device):
        i = self.next
        self.next += 1
        c = pltpu.make_async_remote_copy(
            src_ref=src, dst_ref=dst, send_sem=self.send.at[i], recv_sem=self.recv.at[i],
            device_id=device, device_id_type=MESH,
        )
        c.start()
        return c

    def core_start(self):
        core = self.place["core"]
        self.core_copy = self.copy(self.grad.at[1 - core], self.held, self.place["at"](core=1 - core))

    def core_done(self):
        core = self.place["core"]
        self.core_copy.wait()

        def body(i):
            self.held[i] = (self.held[i].astype(F32) + self.grad[core, i].astype(F32)).astype(BF)

        loop(NY, body)

    def z_start(self):
        place = self.place
        z = place["zh"] * NZL + place["zl"]
        self.z_copies = []
        for j in range(1, NZ):
            there = lax.rem(z + j, NZ)
            zh, zl = there // NZL, lax.rem(there, NZL)
            self.z_copies.append(
                self.copy(self.held.at[place["y"], place["x"], zh, :, rows_of(zl, 128)], self.z.at[j - 1],
                          place["at"](zh=zh, zl=zl))
            )

    def z_done(self):
        place = self.place
        total = self.held[place["y"], place["x"], place["zh"], :, rows_of(place["zl"], 128)].astype(F32)
        for j, c in enumerate(self.z_copies):
            c.wait()
            total = total + self.z[j].astype(F32)
        self.full[place["x"], place["zl"]] = total.astype(BF)

    def gather_start(self):
        place = self.place
        mine = self.full.at[place["x"], place["zl"]]
        slab = place["x"] * NZL + place["zl"]
        self.gather_copies = []
        for j in range(1, N_SLAB):
            there = lax.rem(slab + j, N_SLAB)
            self.gather_copies.append(self.copy(mine, mine, place["at"](x=there // NZL, zl=lax.rem(there, NZL))))

    def gather_done(self):
        for c in self.gather_copies:
            c.wait()

    def matrix(self, tile):
        return [self.full[q, tile].astype(F32) for q in range(NX)]


    def ways(self, stage):
        cut = self.y_first
        ways = [("yx"[stage], pl.ds(0, cut))]
        if cut < NZH:
            ways.append(("xy"[stage], pl.ds(cut, NZH - cut)))
        return ways

    def cross(self, stage, part, axis, i):
        y, x = self.place["y"], self.place["x"]
        if stage == 0:
            return self.held.at[i, :, part] if axis == "y" else self.held.at[:, i, part]
        return self.held.at[i, x, part] if axis == "y" else self.held.at[y, i, part]

    def landing(self, stage, part, j):
        if stage == 0:
            return self.land[0].at[j, :, part]
        return self.land[1].at[j, part]

    def plane_start(self, stage):
        place = self.place
        self.plane = []
        for axis, part in self.ways(stage):
            for j in range(1, 4):
                there = lax.rem(place[axis] + j, 4)
                self.plane.append(
                    self.copy(self.cross(stage, part, axis, there), self.landing(stage, part, j - 1),
                              place["at"](**{axis: there}))
                )

    def plane_done(self, stage):
        for c in self.plane:
            c.wait()
        for axis, part in self.ways(stage):
            add(self.cross(stage, part, axis, self.place[axis]), *[self.landing(stage, part, j) for j in range(3)])


class Gains:
    def __init__(self, refs, place):
        self.sums, self.land, self.send, self.recv = refs
        self.place = place

    def start(self, stage):
        place = self.place
        first = (0, 1, 4, 7)[stage]
        peers = []
        if stage == 0:
            peers = [place["at"](core=1 - place["core"])]
        elif stage < 3:
            axis = "yx"[stage - 1]
            peers = [place["at"](**{axis: lax.rem(place[axis] + j, 4)}) for j in range(1, 4)]
        else:
            z = place["zh"] * NZL + place["zl"]
            for j in range(1, NZ):
                there = lax.rem(z + j, NZ)
                peers.append(place["at"](zh=there // NZL, zl=lax.rem(there, NZL)))
        self.copies = []
        for i, peer in enumerate(peers):
            c = pltpu.make_async_remote_copy(
                src_ref=self.sums.at[stage], dst_ref=self.land.at[first + i], send_sem=self.send.at[first + i],
                recv_sem=self.recv.at[first + i], device_id=peer, device_id_type=MESH,
            )
            c.start()
            self.copies.append(c)

    def done(self, stage):
        first = (0, 1, 4, 7)[stage]
        total = self.sums[stage]
        for i, c in enumerate(self.copies):
            c.wait()
            total = total + self.land[first + i]
        self.sums[stage + 1] = total


def bundle_scratch(tiles):
    c = tiles * 128
    copies = 1 + 6 + 6 + (NZ - 1) + (N_SLAB - 1)
    return [
        pltpu.VMEM((NCORE, NY, NX, NZH, SHARE, c), BF),
        pltpu.VMEM((NY, NX, NZH, SHARE, c), BF),
        pltpu.VMEM((NZ - 1, SHARE, 128), BF),
        pltpu.VMEM((NX, NZL, SHARE, 128), BF),
        pltpu.SemaphoreType.DMA((copies,)),
        pltpu.SemaphoreType.DMA((copies,)),
        pltpu.VMEM((3, 4, NZH, SHARE, c), BF),
        pltpu.VMEM((3, NZH, SHARE, c), BF),
    ]


def kernel(
    lat_in, up_in, wm_in, ws_in, wa_in, wo_in, gains_in, edge_in, nbr_in, sends_in,
    lat_out, grad_out, gm_out, gs_out, ga_out, go_out, gg_out,
    xs, up, wm, ws, wa, wo, gains, edge, nbr, sends, adj, own, xh, mh, out_blocks, back, ret0, ret1,
    pm, pmh, ph, normed, inverse, merged, hidden, acc, acc2, gy, gu, gph, gmg, gpm, gpmh, in_sem, out_sem,
    halo_send, halo_recv, gain_sums, gain_land, gain_send, gain_recv, *bundle_refs,
):
    space = lax.axis_index("space")
    slab = lax.axis_index("slab")
    core = lax.rem(space, NCORE)
    zh = lax.rem(space // NCORE, NZH)
    y = space // (NCORE * NZH)
    zl = lax.rem(slab, NZL)
    x = slab // NZL

    def at(**new):
        p = {"core": core, "zh": zh, "y": y, "zl": zl, "x": x, **new}
        return ((p["y"] * NZH + p["zh"]) * NCORE + p["core"], p["x"] * NZL + p["zl"])

    place = {"core": core, "zh": zh, "y": y, "zl": zl, "x": x, "at": at}
    s_up, s_down = lax.rem(space + 1, N_SPACE), lax.rem(space + N_SPACE - 1, N_SPACE)
    l_up, l_down = lax.rem(slab + 1, N_SLAB), lax.rem(slab + N_SLAB - 1, N_SLAB)
    ahead = [(s_up, slab), (s_down, slab), (space, l_up), (space, l_down)]
    behind = [ahead[1], ahead[0], ahead[3], ahead[2]]

    barrier = pltpu.get_barrier_semaphore()
    partners = list(ahead) + [at(core=1 - core)]
    partners += [at(y=lax.rem(y + j, NY)) for j in range(1, NY)]
    for j in range(1, N_SLAB):
        there = lax.rem(slab + j, N_SLAB)
        partners.append(at(x=there // NZL, zl=lax.rem(there, NZL)))
    z = zh * NZL + zl
    for j in range(1, NZ):
        there = lax.rem(z + j, NZ)
        partners.append(at(zh=there // NZL, zl=lax.rem(there, NZL)))
    for p in partners:
        pl.semaphore_signal(barrier, inc=1, device_id=p, device_id_type=MESH)

    pairs = [
        (lat_in, xs.at[0]), (sends_in.at[0, 0], sends), (wm_in, wm), (nbr_in, nbr), (edge_in, edge), (ws_in, ws),
        (wa_in, wa), (wo_in, wo), (gains_in, gains), (up_in, up),
    ]
    loads = [pltpu.make_async_copy(a, b, in_sem.at[i]) for i, (a, b) in enumerate(pairs)]
    for c in loads:
        c.start()
    lat_load, sends_load, wm_load, nbr_load, edge_load, ws_load, wa_load, wo_load, gains_load, up_load = loads

    count = len(bundle_scratch(1))
    bundles = [Bundle(bundle_refs[i * count : (i + 1) * count], place, Y_FIRST[i // 2])
               for i in range(2 * LAYERS)]
    ret = (ret0, ret1)
    gain = Gains((gain_sums, gain_land, gain_send, gain_recv), place)

    def halo(src, dst, peers, exchange, before):
        copies = {}
        for d in ORDER:
            before(d)
            copies[d] = pltpu.make_async_remote_copy(
                src_ref=src(d), dst_ref=dst(d), send_sem=halo_send.at[exchange, d],
                recv_sem=halo_recv.at[exchange, d], device_id=peers[d], device_id_type=MESH,
            )
            copies[d].start()
        return copies

    def adjacency(e, blocks, rows=slice(None)):
        return jnp.concatenate([adj[e + j, rows] for j in range(blocks)], axis=1)

    def halo_rows(d):
        return slice(d * HALO_ROWS, (d + 1) * HALO_ROWS)

    def picked(l):
        def pick(d):
            for t in range(2):
                out_blocks[l, d, block_rows(t)] = xs[l, sends[t, d]]

        return pick

    lat_load.wait()
    sends_load.wait()
    pl.semaphore_wait(barrier, len(partners))
    wide = [slice(i * 256, (i + 1) * 256) for i in range(ROWS // 256)]

    def update_grad(l, cotangent):
        row = jnp.zeros((1, W), F32)
        for r in wide:
            g = cotangent(r)
            n = normed[l, r]
            row = row + jnp.sum(g * n, axis=0, keepdims=True)
            g = g * gains[l : l + 1, :]
            u = g - jnp.mean(g, axis=-1, keepdims=True) - n * jnp.mean(g * n, axis=-1, keepdims=True)
            gu[l, r] = (inverse[l, r] * u).astype(BF)
        for r in wide:
            gph[l, r] = (dot(gu[l, r], wo[l], 1, 1) * ph[l, r]).astype(BF)
        for r in wide:
            gmg[r] = dot(gph[l, r], wa[l], 1, 1).astype(BF)
        gain_sums[0, l : l + 1, :] = row

    for l in range(LAYERS):
        copies = halo(
            lambda d: out_blocks.at[l, d], lambda d: xh.at[l, pl.ds(d * HALO_ROWS, HALO_ROWS)], ahead, l, picked(l)
        )
        if l == 0:
            wm_load.wait()
        for b in range(OWN):
            r = block_rows(b)
            v = dot(xs[l, b], wm[l], 1, 0)
            s = sigmoid(v)
            own[r] = (v * s).astype(BF)
            pm[l, r] = slope(v, s)
        if l == 0:
            edge_load.wait()
            nbr_load.wait()

            def build(i):
                b = i // SLOTS
                e = lax.rem(i, SLOTS)
                total = jnp.zeros((BLOCK, BLOCK), F32)
                for k in range(TILES):
                    keep = jnp.where(nbr[b, k] == e, 1.0, 0.0)
                    total = total + edge[b, k].astype(F32) * keep
                adj[e, rows_of(b, BLOCK), :] = total.astype(BF)

            loop(OWN * SLOTS, build)
            for c in (ws_load, wa_load, wo_load, gains_load, up_load):
                c.wait()
        for b in range(OWN):
            r = block_rows(b)
            ph[l, r] = dot(xs[l, b], ws[l], 1, 0)
            acc[r] = dot(adjacency(0, OWN, r), own[...], 1, 0)
        if l > 0:
            for i in range(4 * HALO_ROWS // BLOCK):
                r = block_rows(i)
                v = pmh[l - 1, r]
                pmh[l - 1, r] = slope(v, sigmoid(v))
        for d in ORDER_IN:
            copies[d].wait()
            for t in range(2):
                r = slice(d * HALO_ROWS + t * BLOCK, d * HALO_ROWS + (t + 1) * BLOCK)
                v = dot(xh[l, r], wm[l], 1, 0)
                pmh[l, r] = v
                mh[r] = (v * sigmoid(v)).astype(BF)
            if d != ORDER_IN[-1]:
                for b in range(OWN):
                    r = block_rows(b)
                    acc[r] += dot(adjacency(OWN + 2 * d, 2, r), mh[halo_rows(d)], 1, 0)
        d = ORDER_IN[-1]
        last = mh[halo_rows(d)]
        for b in range(OWN):
            r = block_rows(b)
            merged[l, r] = (acc[r] + dot(adjacency(OWN + 2 * d, 2, r), last, 1, 0)).astype(BF)
        for b in range(OWN):
            r = block_rows(b)
            v = ph[l, r] + dot(merged[l, r], wa[l], 1, 0)
            s = sigmoid(v)
            hidden[l, r] = (v * s).astype(BF)
            ph[l, r] = slope(v, s)
        updates = [dot(hidden[l, block_rows(b)], wo[l], 1, 0) for b in range(OWN)]
        for b, u in enumerate(updates):
            r = block_rows(b)
            centred = u - jnp.mean(u, axis=-1, keepdims=True)
            inv = lax.rsqrt(jnp.mean(centred * centred, axis=-1, keepdims=True) + EPS)
            n = centred * inv
            xs[l + 1, b] = (xs[l, b].astype(F32) + gains[l : l + 1, :] * n).astype(BF)
            normed[l, r] = n
            inverse[l, r] = inv

    update_grad(LAYERS - 1, lambda r: up[r].astype(F32))
    out_copy = pltpu.make_async_copy(xs.at[LAYERS], lat_out, out_sem.at[0])
    out_copy.start()

    def weight_grad(bundle, tile, *pairs):
        for i in range(2):
            r = pl.ds(i * 256, 256)
            v = sum(dot(a(r), g[...], 0, 0) for a, g in pairs)
            v = v.astype(BF).reshape(2, NZH, NCORE, SHARE, W)
            for c in range(NCORE):
                for q in range(NX):
                    bundle.grad[c, pl.ds(2 * i, 2), q, :, :, tile * 128 : (tile + 1) * 128] = v[
                        :, :, c, :, q * 128 : (q + 1) * 128
                    ]

    def put(out, l, bundle, tile):
        for q, v in enumerate(bundle.matrix(tile)):
            out[l, :, q * 128 : (q + 1) * 128] = v

    def put_gains():
        pick = lax.broadcasted_iota(jnp.int32, (W, SHARE), 0) - space * SHARE
        pick = (pick == lax.broadcasted_iota(jnp.int32, (W, SHARE), 1)).astype(F32)
        gg_out[...] = lax.dot_general(
            gain_sums[4], pick, (((1,), (0,)), ((), ())), precision=lax.Precision.HIGHEST, preferred_element_type=F32
        )

    def put_all(l, one, two):
        one.gather_done()
        put(go_out, l, one, 0)
        put(gs_out, l, one, 1)
        two.gather_done()
        put(ga_out, l, two, 0)
        put(gm_out, l, two, 1)

    def z_to_gather(one, two):
        for bundle in (one, two):
            bundle.z_done()
            bundle.gather_start()

    earlier = None
    for l in reversed(range(LAYERS)):

        def back_grad(d, l=l):
            v = dot(adjacency(OWN + 2 * d, 2), gmg[...], 0, 0)
            back[l, d] = v.astype(BF).reshape(2, BLOCK, W)

        one, two = bundles[2 * l], bundles[2 * l + 1]

        def latent_columns(r, l=l):
            return xs[l, :, :, r].reshape(ROWS, 256)

        def first_grads(l=l):
            weight_grad(one, 0, (lambda r: hidden[l, :, r], gu.at[l]))
            weight_grad(one, 1, (latent_columns, gph.at[l]))
            one.core_start()

        if l == 0:
            first_grads()
            gain.start(0)
        copies = halo(
            lambda d: back.at[l, d], lambda d: ret[l].at[d, pl.ds(0, 2)], behind, LAYERS + l, back_grad
        )

        if l > 0:
            first_grads()
        for b in range(OWN):
            r = block_rows(b)
            v = dot(adj[b], gmg[...], 0, 0)
            acc2[r] = v
            gpm[r] = (v * pm[l, r]).astype(BF)
        for i in range(4 * HALO_ROWS // BLOCK):
            r = block_rows(i)
            v = pmh[l, r]
            if l == LAYERS - 1:
                v = slope(v, sigmoid(v))
            gpmh[r] = (back[l, i // 2, i % 2].astype(F32) * v).astype(BF)
        weight_grad(two, 0, (lambda r: merged[l, :, r], gph.at[l]))
        weight_grad(two, 1, (latent_columns, gpm), (lambda r: xh[l, :, r], gpmh))
        two.core_start()
        one.core_done()
        one.plane_start(0)
        if earlier:
            for bundle in earlier:
                bundle.plane_done(0)
                bundle.plane_start(1)
            gain.done(0)
            gain.start(1)
        for b in range(OWN):
            r = block_rows(b)
            before = up[r].astype(F32) if l == LAYERS - 1 else gy[r]
            gy[r] = before + dot(gph[l, r], ws[l], 1, 1)
        for d in range(4):
            ret[l][d, 2] = jnp.zeros((BLOCK, W), BF)
        two.core_done()
        two.plane_start(0)
        if earlier:
            one.plane_done(0)
            one.plane_start(1)
            gain.done(1)
            gain.start(2)
            two.plane_done(0)
            two.plane_start(1)
            gain.done(2)
            gain.start(3)
            one.plane_done(1)
            one.z_start()
            two.plane_done(1)
            two.z_start()
            for bundle in earlier:
                bundle.plane_done(1)
                bundle.z_start()
        for d in ORDER:
            copies[d].wait()

        def message_grad(b, l=l):
            r = block_rows(b)
            total = acc2[r]
            for d in range(4):
                which = jnp.where(sends[0, d] == b, 0, jnp.where(sends[1, d] == b, 1, 2))
                total = total + ret[l][d, which].astype(F32)
            gpm[r] = (total * pm[l, r]).astype(BF)

        for b in range(OWN):
            message_grad(b)
        for r in wide:
            gy[r] += dot(gpm[r], wm[l], 1, 1)
        if l > 0:
            update_grad(l - 1, lambda r: gy[r])
        earlier = (one, two)

    grad_copy = pltpu.make_async_copy(gy, grad_out, out_sem.at[1])
    grad_copy.start()
    gain.done(3)
    z_to_gather(*earlier)
    z_to_gather(*bundles[2 * LAYERS - 2 :])
    put_gains()
    put_all(0, *earlier)
    put_all(LAYERS - 1, *bundles[2 * LAYERS - 2 :])
    out_copy.wait()
    grad_copy.wait()


PIECES = (2, 4, 1, 1, 1, 1, 1)


def hand_over(*refs):
    count = len(PIECES)
    into, out, held = refs[:count], refs[count : 2 * count], refs[2 * count : 3 * count]
    in_sem, out_sem = refs[3 * count :]
    steps = []
    for i, pieces in enumerate(PIECES):
        size = into[i].shape[0] // pieces
        for j in range(pieces):
            piece = pl.ds(j * size, size)
            n = len(steps)
            steps.append((
                pltpu.make_async_copy(into[i].at[piece], held[i].at[piece], in_sem.at[n]),
                pltpu.make_async_copy(held[i].at[piece], out[i].at[piece], out_sem.at[n]),
            ))
    for first, _ in steps:
        first.start()
    for first, second in steps:
        first.wait()
        second.start()
    for _, second in steps:
        second.wait()


def local(
    latents, upstream, msg_weight, self_weight, agg_weight, out_weight, gains, edge_weight, nbr_slot, send_list
):
    hbm = pl.BlockSpec(memory_space=pl.ANY)
    vmem = pl.BlockSpec(memory_space=pltpu.VMEM)
    share = jax.ShapeDtypeStruct((LAYERS, SHARE, W), F32)
    scratch = [
        pltpu.VMEM((LAYERS + 1, OWN, BLOCK, W), BF),
        pltpu.VMEM((ROWS, W), BF),
        pltpu.VMEM((LAYERS, W, W), BF),
        pltpu.VMEM((LAYERS, W, W), BF),
        pltpu.VMEM((LAYERS, W, W), BF),
        pltpu.VMEM((LAYERS, W, W), BF),
        pltpu.VMEM((LAYERS, W), F32),
        pltpu.VMEM((OWN, TILES, BLOCK, BLOCK), BF),
        pltpu.SMEM((OWN, TILES), jnp.int32),
        pltpu.SMEM((2, 4), jnp.int32),
        pltpu.VMEM((SLOTS, ROWS, BLOCK), BF),
        pltpu.VMEM((ROWS, W), BF),
        pltpu.VMEM((LAYERS, 4 * HALO_ROWS, W), BF),
        pltpu.VMEM((4 * HALO_ROWS, W), BF),
        pltpu.VMEM((LAYERS, 4, HALO_ROWS, W), BF),
        pltpu.VMEM((LAYERS, 4, 2, BLOCK, W), BF),
        pltpu.VMEM((4, 3, BLOCK, W), BF),
        pltpu.VMEM((4, 3, BLOCK, W), BF),
        pltpu.VMEM((LAYERS, ROWS, W), F32),
        pltpu.VMEM((LAYERS, 4 * HALO_ROWS, W), F32),
        pltpu.VMEM((LAYERS, ROWS, W), F32),
        pltpu.VMEM((LAYERS, ROWS, W), F32),
        pltpu.VMEM((LAYERS, ROWS, 1), F32),
        pltpu.VMEM((LAYERS, ROWS, W), BF),
        pltpu.VMEM((LAYERS, ROWS, W), BF),
        pltpu.VMEM((ROWS, W), F32),
        pltpu.VMEM((ROWS, W), F32),
        pltpu.VMEM((ROWS, W), F32),
        pltpu.VMEM((LAYERS, ROWS, W), BF),
        pltpu.VMEM((LAYERS, ROWS, W), BF),
        pltpu.VMEM((ROWS, W), BF),
        pltpu.VMEM((ROWS, W), BF),
        pltpu.VMEM((4 * HALO_ROWS, W), BF),
        pltpu.SemaphoreType.DMA((10,)),
        pltpu.SemaphoreType.DMA((2,)),
        pltpu.SemaphoreType.DMA((2 * LAYERS, 4)),
        pltpu.SemaphoreType.DMA((2 * LAYERS, 4)),
        pltpu.VMEM((5, LAYERS, W), F32),
        pltpu.VMEM((14, LAYERS, W), F32),
        pltpu.SemaphoreType.DMA((14,)),
        pltpu.SemaphoreType.DMA((14,)),
    ]
    for tiles in BUNDLE_TILES * LAYERS:
        scratch += bundle_scratch(tiles)
    shapes = (
        jax.ShapeDtypeStruct((OWN, BLOCK, W), BF),
        jax.ShapeDtypeStruct((ROWS, W), F32),
        share, share, share, share,
        jax.ShapeDtypeStruct((LAYERS, SHARE), F32),
    )
    out = pl.pallas_call(
        kernel,
        out_shape=shapes,
        in_specs=[hbm] * 10,
        out_specs=(hbm, hbm, vmem, vmem, vmem, vmem, vmem),
        scratch_shapes=scratch,
        compiler_params=pltpu.CompilerParams(
            collective_id=0, has_side_effects=True, vmem_limit_bytes=60 * 1024 * 1024
        ),
        cost_estimate=pl.CostEstimate(flops=10 * 10**9, bytes_accessed=10 * 2**20, transcendentals=2 * 10**6),
    )(latents.reshape(OWN, BLOCK, W), upstream, msg_weight, self_weight, agg_weight, out_weight, gains, edge_weight, nbr_slot, jnp.swapaxes(send_list, 2, 3))
    first, *rest = pl.pallas_call(
        hand_over,
        out_shape=shapes,
        in_specs=[hbm] * 7,
        out_specs=[hbm] * 7,
        scratch_shapes=[pltpu.VMEM(v.shape, v.dtype) for v in shapes]
        + [pltpu.SemaphoreType.DMA((sum(PIECES),)), pltpu.SemaphoreType.DMA((sum(PIECES),))],
    )(*out)
    return (first.reshape(ROWS, W), *rest)


def solution(mesh):
    rows = P(("space", "slab"), None)
    return jax.shard_map(
        local,
        mesh=mesh,
        in_specs=(
            rows, rows, P(), P(), P(), P(), P(),
            P(("space", "slab"), None, None, None), rows, P("space", "slab", None, None),
        ),
        out_specs=(
            rows, rows, P(None, "space", None), P(None, "space", None), P(None, "space", None),
            P(None, "space", None), P(None, "space"),
        ),
        check_vma=False,
    )
```
